32 devices in a mesh: row: 4 (over y, core), col: 8 (over z, x).
Axes of the slice: x: 2, y: 2, z: 4, core: 2. Of those that a mesh axis runs over, the one named last changes fastest.
Arguments:
- traces: float32 [64, 4096], P(('row', 'col')), may hold values from -6 to 6
- offsets: int32 [64, 8], P(('row', 'col')), may hold values from 0 to 3072, as said below
- band_lo: int32 [64], P(('row', 'col')), may hold values from 0 to 63
- band_hi: int32 [64], P(('row', 'col')), may hold values from 192 to 256
- live: int32 [64], P(('row', 'col')), may hold values 0 or 1
Outputs:
- correlations: bfloat16 [64, 8, 4, 2, 512], P('row', 'col')
The draws below stay inside these ranges and needn't reach their ends.
Inputs may be any that keep to these rules, and one draw needn't show every extreme that they name: `offsets`: every offset is a multiple of 256.
All inputs are finite; a program needn't handle non-finite values. No bound on the sum of `live` on one device may be relied on, other than what follows from the above.
Results may differ from the reference program's by a relative error of at most 0.0052.
Values may be sent and summed in bfloat16 or wider, within the bound.
No kernel may reach another device: no remote copies, remote signals or barrier semaphores. Data moves between devices by JAX's collectives and lax.ppermute only.
A program may use at most 64 MiB of HBM per device.

```python
import math
import jax
import jax.numpy as jnp
from jax import lax

CH_DEV = 2
SEG = 8
SAMPLES = 1024
BINS = 256
LAGS = 512
TRACE = 4096
CHANNELS = 64
ROW_PANEL = 16
N_ROW = 4
N_COL = 8


def draw_offsets(key, part):
    quarter = SAMPLES // 4
    steps_count = (TRACE - SAMPLES) // quarter + 1
    return (quarter * jax.random.randint(key, (CHANNELS, SEG), 0, steps_count)).astype(jnp.int32)


def with_ends(drawn, own_key, least, high):
    longest = drawn.shape.index(max(drawn.shape))
    spots = []
    for shift in (0, 1):
        where = [jax.random.randint(jax.random.fold_in(own_key, axis), (), 0, length) for axis, length in enumerate(drawn.shape)]
        where[longest] = (where[longest] + shift) % drawn.shape[longest]
        spots.append(tuple(where))
    return drawn.at[spots[0]].set(least).at[spots[1]].set(high)


def level_of(stream_key, extent, split, least, high):
    level = 1.0
    for position, parts in split:
        heights = jax.random.uniform(jax.random.fold_in(jax.random.fold_in(stream_key, 6), position), (parts,), jnp.float32, least / len(split), high / len(split))
        level = level * jnp.repeat(jnp.exp(heights), extent[position] // parts).reshape((-1,) + (1,) * (len(extent) - 1 - position))
    return level


def normal_values(stream_key, extent, deviation, limit, cuts=(), kind=jnp.bfloat16):
    drawn = jax.random.normal(stream_key, extent, jnp.float32) * deviation
    if len(cuts) > 0:
        drawn = level_of(stream_key, extent, cuts, -0.22, 0.18) * drawn
    return jnp.clip(drawn, min=-limit, max=limit).astype(kind)


def setup_inputs(seed: int = 0) -> dict:
    key_of = jax.random.split(jax.random.key(seed), 6)
    traces = normal_values(key_of[0], (CHANNELS, TRACE), 1.0, 6.0, ((0, 32),), jnp.float32)
    offsets = draw_offsets(jax.random.fold_in(key_of[5], 71), 0)
    band_lo = with_ends(jax.random.randint(key_of[2], (CHANNELS,), 0, BINS // 4), jax.random.fold_in(key_of[2], 1), 0, (BINS // 4) - 1).astype(jnp.int32)
    band_hi = with_ends(jax.random.randint(key_of[3], (CHANNELS,), 3 * BINS // 4, BINS + 1), jax.random.fold_in(key_of[3], 1), 3 * BINS // 4, BINS).astype(jnp.int32)
    live = with_ends((jax.random.randint(key_of[4], (CHANNELS,), 0, 16) < 15).astype(jnp.int32), jax.random.fold_in(key_of[4], 1), 0, 1)
    return dict(traces=traces, offsets=offsets, band_lo=band_lo, band_hi=band_hi, live=live)


def transform_table():
    times = jnp.arange(SAMPLES, dtype=jnp.int32)
    freqs = jnp.arange(BINS, dtype=jnp.int32) + 1
    phase = jnp.mod(times[:, None] * freqs[None, :], SAMPLES).astype(jnp.float32) * (2.0 * math.pi / SAMPLES)
    taper = 0.5 - 0.5 * jnp.cos(times.astype(jnp.float32) * (2.0 * math.pi / SAMPLES))
    return jnp.concatenate([jnp.cos(phase), -jnp.sin(phase)], axis=1) * taper[:, None]

def lag_table():
    freqs = jnp.arange(BINS, dtype=jnp.int32) + 1
    shifts = jnp.arange(LAGS, dtype=jnp.int32) - LAGS // 2
    phase = jnp.mod(freqs[:, None] * shifts[None, :], SAMPLES).astype(jnp.float32) * (2.0 * math.pi / SAMPLES)
    return jnp.concatenate([jnp.cos(phase), -jnp.sin(phase)], axis=0) * (1.0 / math.sqrt(SEG * BINS))

def whiten(traces, offsets, band_lo, band_hi, live):

    def cut_one(record, start):
        return lax.dynamic_slice_in_dim(record, start, SAMPLES)

    def cut_channel(record, starts):
        return jax.vmap(cut_one, in_axes=(None, 0))(record, starts.astype(jnp.int32))
    segment = jax.vmap(cut_channel)(traces, offsets)
    count = traces.shape[0]
    flat = segment.reshape(count * SEG, SAMPLES)
    spec = jnp.dot(flat, transform_table(), precision=lax.Precision.HIGHEST)
    spec_re = spec[:, :BINS]
    spec_im = spec[:, BINS:]
    amp = jnp.sqrt(spec_re * spec_re + spec_im * spec_im)
    padded = jnp.pad(amp, ((0, 0), (2, 2)))
    smooth = (padded[:, 0:BINS] + padded[:, 1:BINS + 1] + padded[:, 2:BINS + 2] + padded[:, 3:BINS + 3] + padded[:, 4:BINS + 4]) / 5.0
    level = lax.optimization_barrier(jnp.mean(amp, axis=1, keepdims=True))
    factor = 1.0 / (smooth + 0.1 * level + 1e-06)
    bins = jnp.arange(BINS, dtype=jnp.int32)
    inside = (bins[None, :] >= band_lo[:, None]) & (bins[None, :] < band_hi[:, None]) & (live[:, None] == 1)
    keep = inside.astype(jnp.float32)
    factor = factor.reshape(count, SEG, BINS) * keep[:, None, :]
    spec = spec.reshape(count, SEG, 2 * BINS)
    white = spec * jnp.concatenate([factor, factor], axis=2)
    return white.astype(jnp.bfloat16)

def correlate(first, second, table):
    first = first.astype(jnp.float32)
    second = second.astype(jnp.float32)
    first_re, first_im = (first[..., :BINS], first[..., BINS:])
    second_re, second_im = (second[..., :BINS], second[..., BINS:])
    cross_re = jnp.einsum('isb,jsb->ijb', first_re, second_re) + jnp.einsum('isb,jsb->ijb', first_im, second_im)
    cross_im = jnp.einsum('isb,jsb->ijb', first_im, second_re) - jnp.einsum('isb,jsb->ijb', first_re, second_im)
    cross = jnp.concatenate([cross_re, cross_im], axis=2)
    count_i, count_j = (cross.shape[0], cross.shape[1])
    corr = jnp.dot(cross.reshape(count_i * count_j, 2 * BINS), table, precision=lax.Precision.HIGHEST)
    return corr.astype(jnp.bfloat16).reshape(count_i, count_j, LAGS)

def reference(traces, offsets, band_lo, band_hi, live):
    white = whiten(traces, offsets, band_lo, band_hi, live)
    columns = white.reshape(N_ROW, N_COL, CH_DEV, SEG, 2 * BINS).transpose(1, 0, 2, 3, 4).reshape(CHANNELS, SEG, 2 * BINS)
    panels = white.reshape(N_ROW, ROW_PANEL, SEG, 2 * BINS)
    table = lag_table()

    def one_panel(panel):
        return correlate(panel, columns, table)
    result = lax.map(one_panel, panels)
    return result.reshape(CHANNELS, N_COL, N_ROW, CH_DEV, LAGS)
```

```python
import functools
import math

import jax
import jax.numpy as jnp
import numpy as np
from jax import lax
from jax.experimental import pallas as pl
from jax.experimental.pallas import tpu as pltpu
from jax.sharding import PartitionSpec as P

SEG = 8
SAMPLES = 1024
BINS = 256
LAGS = 512
TRACE = 4096
QUARTER = SAMPLES // 4
BLOCKS = TRACE // QUARTER
LANES = 128
VMEM = pl.BlockSpec(memory_space=pltpu.VMEM)
SMEM = pl.BlockSpec(memory_space=pltpu.SMEM)


def split(values):
    high = values.astype(jnp.bfloat16)
    return high, (values - high.astype(jnp.float32)).astype(jnp.bfloat16)


def split_table(table):
    high = table.astype(jnp.bfloat16)
    return np.stack([high, (table - high.astype(np.float64)).astype(jnp.bfloat16)])


def quarter_table():
    times = np.arange(QUARTER)
    freqs = np.arange(BINS) + 1
    phase = (times[:, None] * freqs[None, :] % SAMPLES) * (2.0 * math.pi / SAMPLES)
    return split_table(np.concatenate([np.cos(phase), -np.sin(phase)], axis=1))


def wave_rows():
    turn = np.arange(QUARTER) * (2.0 * math.pi / SAMPLES)
    freqs = np.arange(BINS) + 1
    cos_turn = np.array([1.0, 0.0, -1.0, 0.0])[freqs % 4]
    sin_turn = np.array([0.0, 1.0, 0.0, -1.0])[freqs % 4]
    rows = np.zeros((8, QUARTER), np.float32)
    rows[0] = np.cos(turn)
    rows[1] = np.sin(turn)
    rows[2] = cos_turn
    rows[3] = sin_turn
    rows[4] = np.where(freqs % 2 == 0, 1.0, -1.0)
    return rows


def lag_table():
    freqs = np.arange(BINS) + 1
    shifts = np.arange(LAGS) - LAGS // 2
    phase = (freqs[:, None] * shifts[None, :] % SAMPLES) * (2.0 * math.pi / SAMPLES)
    table = np.concatenate([np.cos(phase), -np.sin(phase)], axis=0)
    return split_table(table / math.sqrt(SEG * BINS))


def dot(left, right):
    return jnp.dot(left, right, preferred_element_type=jnp.float32)


def dot_split(values, table_ref):
    high, low = split(values)
    return dot(high, table_ref[0]) + (dot(low, table_ref[0]) + dot(high, table_ref[1]))


def whiten_kernel(offsets, band_lo, band_hi, live, traces, table, waves, out, quarters, white):
    count = traces.shape[0]
    rows = count * BLOCKS
    for k in range(count):
        for block in range(BLOCKS):
            quarters[pl.ds(k * BLOCKS + block, 1), :] = traces[
                pl.ds(k, 1), pl.ds(block * QUARTER, QUARTER)
            ]
    plain = quarters[...] * 0.5
    spectra = dot_split(
        jnp.concatenate([plain, plain * waves[0:1, :], plain * waves[1:2, :]], axis=0), table
    )
    flat, with_cos, with_sin = (spectra[n * rows : (n + 1) * rows] for n in range(3))

    def later(values, steps):
        return pltpu.roll(values, rows - steps, 0)

    first = flat - with_cos
    second = later(flat + with_sin, 1)
    third = later(flat + with_cos, 2)
    fourth = later(flat - with_sin, 3)
    cos_turn, sin_turn, sign = waves[2:3, :], waves[3:4, :], waves[4:5, :]
    both = second + fourth
    diff = second - fourth
    re = (
        first[:, :BINS]
        + third[:, :BINS] * sign
        + (both[:, :BINS] * cos_turn + diff[:, BINS:] * sin_turn)
    )
    im = (
        first[:, BINS:]
        + third[:, BINS:] * sign
        + (both[:, BINS:] * cos_turn - diff[:, :BINS] * sin_turn)
    )
    amp = jnp.sqrt(re * re + im * im)
    bins = lax.broadcasted_iota(jnp.int32, (1, BINS), 1)
    total = amp
    for step in (1, 2):
        total = total + jnp.where(bins >= step, pltpu.roll(amp, step, 1), 0.0)
        total = total + jnp.where(bins < BINS - step, pltpu.roll(amp, BINS - step, 1), 0.0)
    level = jnp.sum(amp, axis=1, keepdims=True) * (1.0 / BINS)
    factor = 1.0 / (total / 5.0 + 0.1 * level + 1e-06)
    keep = jnp.concatenate(
        [
            jnp.broadcast_to(
                jnp.where(
                    (bins >= band_lo[k]) & (bins < jnp.where(live[k] == 1, band_hi[k], 0)), 1.0, 0.0
                ),
                (BLOCKS, BINS),
            )
            for k in range(count)
        ],
        axis=0,
    )
    factor = factor * keep
    re, im = re * factor, im * factor
    for t in range(BINS // LANES):
        white[t] = re[:, t * LANES : (t + 1) * LANES]
        white[t + BINS // LANES] = im[:, t * LANES : (t + 1) * LANES]
    for t in range(2 * BINS // LANES):
        picked = [
            white[t, pl.ds(k * BLOCKS + lax.div(offsets[k, s], QUARTER), 1), :]
            for k in range(count)
            for s in range(SEG)
        ]
        out[:, t * LANES : (t + 1) * LANES] = jnp.concatenate(picked, axis=0).astype(jnp.bfloat16)


def whiten(traces, offsets, band_lo, band_hi, live):
    count = traces.shape[0]
    rows = count * BLOCKS
    return pl.pallas_call(
        whiten_kernel,
        out_shape=jax.ShapeDtypeStruct((count * SEG, 2 * BINS), jnp.bfloat16),
        in_specs=[SMEM] * 4 + [VMEM] * 3,
        out_specs=VMEM,
        scratch_shapes=[
            pltpu.VMEM((rows, QUARTER), jnp.float32),
            pltpu.VMEM((2 * BINS // LANES, rows, LANES), jnp.float32),
        ],
        name="whiten",
    )(offsets, band_lo, band_hi, live, traces, jnp.asarray(quarter_table()), jnp.asarray(wave_rows()))


def correlate_kernel(count, first_masks, second_masks, *refs):
    n_first, n_second = len(first_masks), len(second_masks)
    first_refs, second_refs = refs[:n_first], refs[n_first : n_first + n_second]
    table, out, left, right, cross = refs[n_first + n_second :]
    wide = count * n_second
    for n, ref in enumerate(second_refs):
        for k in range(count):
            rows = ref[k * SEG : (k + 1) * SEG, :].astype(jnp.float32)
            for t in range(2 * BINS // LANES):
                right[t, pl.ds(n * count + k, SEG, stride=wide), :] = rows[
                    :, t * LANES : (t + 1) * LANES
                ]
    at = 0
    for ref in first_refs:
        left[at : at + ref.shape[0], :] = ref[...].astype(jnp.float32)
        at += ref.shape[0]
    channels = at // SEG

    @pl.loop(0, channels, unroll=4)
    def _(i):
        there = pl.ds(pl.multiple_of(i * wide, wide), wide)
        segments = pl.ds(pl.multiple_of(i * SEG, SEG), SEG)
        for t in range(BINS // LANES):
            re = pl.ds(t * LANES, LANES)
            im = pl.ds(BINS + t * LANES, LANES)
            cross_re = jnp.zeros((wide, LANES), jnp.float32)
            cross_im = jnp.zeros((wide, LANES), jnp.float32)
            rows_re, rows_im = left[segments, re], left[segments, im]
            for s in range(SEG):
                left_re, left_im = rows_re[s : s + 1, :], rows_im[s : s + 1, :]
                right_re = right[t, s * wide : (s + 1) * wide, :]
                right_im = right[t + BINS // LANES, s * wide : (s + 1) * wide, :]
                cross_re = cross_re + (left_re * right_re + left_im * right_im)
                cross_im = cross_im + (left_im * right_re - left_re * right_im)
            cross[there, re] = cross_re
            cross[there, im] = cross_im

    row_index, col_index = lax.axis_index("row"), lax.axis_index("col")
    at = 0
    for masks in first_masks:
        for mask in masks:
            size = count * wide
            corr = dot_split(cross[at : at + size, :], table).astype(jnp.bfloat16)
            at += size
            for k in range(count):
                for n, row_mask in enumerate(second_masks):
                    start = k * wide + n * count
                    out[(col_index ^ mask) * count + k, 0, row_index ^ row_mask] = corr[
                        start : start + count, :
                    ]


def correlate(count, n_row, n_col, first, second):
    first_masks = tuple(tuple(masks) for masks, _ in first)
    second_masks = tuple(mask for masks, _ in second for mask in masks)
    channels, wide = count * n_col, count * n_row
    return pl.pallas_call(
        functools.partial(correlate_kernel, count, first_masks, second_masks),
        out_shape=jax.ShapeDtypeStruct((channels, 1, n_row, count, LAGS), jnp.bfloat16),
        in_specs=[VMEM] * (len(first) + len(second) + 1),
        out_specs=VMEM,
        scratch_shapes=[
            pltpu.VMEM((channels * SEG, 2 * BINS), jnp.float32),
            pltpu.VMEM((2 * BINS // LANES, wide * SEG, LANES), jnp.float32),
            pltpu.VMEM((channels * wide, 2 * BINS), jnp.float32),
        ],
        name="correlate",
    )(*(a for _, a in first), *(a for _, a in second), jnp.asarray(lag_table()))


def swap(block, axis, mask):
    return lax.ppermute(block, axis, [(i, i ^ mask) for i in range(lax.axis_size(axis))])


def body(traces, offsets, band_lo, band_hi, live):
    count = traces.shape[0]
    n_row, n_col = lax.axis_size("row"), lax.axis_size("col")
    white = whiten(traces, offsets, band_lo, band_hi, live)
    second = [([0], white)]
    bit = n_row // 2
    while bit:
        second += [([masks[0] ^ bit], swap(block, "row", bit)) for masks, block in second]
        bit //= 2
    held, masks = white, [0]
    bit = n_col // 2
    while bit > 2:
        held = jnp.concatenate([held, swap(held, "col", bit)], axis=0)
        masks = masks + [mask ^ bit for mask in masks]
        bit //= 2
    first = [(masks, held)]
    for step in (3, 1, 2):
        if step < n_col:
            first.append(([mask ^ step for mask in masks], swap(held, "col", step)))
    return correlate(count, n_row, n_col, first, second)


def solution(mesh):
    in_specs = (
        P(("row", "col"), None),
        P(("row", "col"), None),
        P(("row", "col")),
        P(("row", "col")),
        P(("row", "col")),
    )
    out_specs = P("row", "col", None, None, None)
    return jax.shard_map(body, mesh=mesh, in_specs=in_specs, out_specs=out_specs, check_vma=False)
```

```python
import functools
import math

import jax
import jax.numpy as jnp
import numpy as np
from jax import lax
from jax.experimental import pallas as pl
from jax.experimental.pallas import tpu as pltpu
from jax.sharding import PartitionSpec as P

SEG = 8
SAMPLES = 1024
BINS = 256
LAGS = 512
TRACE = 4096
QUARTER = SAMPLES // 4
BLOCKS = TRACE // QUARTER
LANES = 128
VMEM = pl.BlockSpec(memory_space=pltpu.VMEM)
SMEM = pl.BlockSpec(memory_space=pltpu.SMEM)


def split(values):
    high = values.astype(jnp.bfloat16)
    return high, (values - high.astype(jnp.float32)).astype(jnp.bfloat16)


def split_table(table):
    high = table.astype(jnp.bfloat16)
    return np.stack([high, (table - high.astype(np.float64)).astype(jnp.bfloat16)])


def quarter_table():
    times = np.arange(QUARTER)
    freqs = np.arange(BINS) + 1
    phase = (times[:, None] * freqs[None, :] % SAMPLES) * (2.0 * math.pi / SAMPLES)
    return split_table(np.concatenate([np.cos(phase), -np.sin(phase)], axis=1))


def wave_rows():
    turn = np.arange(QUARTER) * (2.0 * math.pi / SAMPLES)
    freqs = np.arange(BINS) + 1
    cos_turn = np.array([1.0, 0.0, -1.0, 0.0])[freqs % 4]
    sin_turn = np.array([0.0, 1.0, 0.0, -1.0])[freqs % 4]
    rows = np.zeros((8, QUARTER), np.float32)
    rows[0] = np.cos(turn)
    rows[1] = np.sin(turn)
    rows[2] = cos_turn
    rows[3] = sin_turn
    rows[4] = np.where(freqs % 2 == 0, 1.0, -1.0)
    return rows


def lag_table():
    freqs = np.arange(BINS) + 1
    shifts = np.arange(LAGS) - LAGS // 2
    phase = (freqs[:, None] * shifts[None, :] % SAMPLES) * (2.0 * math.pi / SAMPLES)
    table = np.concatenate([np.cos(phase), -np.sin(phase)], axis=0)
    return split_table(table / math.sqrt(SEG * BINS))


def in_vmem(array):
    return pltpu.with_memory_space_constraint(array, pltpu.VMEM)


def dot(left, right):
    return jnp.dot(left, right, preferred_element_type=jnp.float32)


def dot_split(values, table_ref):
    high, low = split(values)
    return dot(high, table_ref[0]) + (dot(low, table_ref[0]) + dot(high, table_ref[1]))


def whiten_kernel(
    offsets_in, band_lo_in, band_hi_in, live_in, traces_in, waves_in, table_in, lags_in,
    out, lags_out,
    offsets, band_lo, band_hi, live, traces, waves, table, quarters, white, arrived,
):
    sources = (traces_in, waves_in, table_in, offsets_in, band_lo_in, band_hi_in, live_in, lags_in)
    targets = (traces, waves, table, offsets, band_lo, band_hi, live, lags_out)
    copies = [
        pltpu.make_async_copy(source, target, arrived.at[n])
        for n, (source, target) in enumerate(zip(sources, targets, strict=True))
    ]
    for copy in copies:
        copy.start()
    count = traces.shape[0]
    copies[0].wait()
    rows = count * BLOCKS
    for k in range(count):
        for block in range(BLOCKS):
            quarters[pl.ds(k * BLOCKS + block, 1), :] = traces[
                pl.ds(k, 1), pl.ds(block * QUARTER, QUARTER)
            ]
    plain = quarters[...] * 0.5
    copies[1].wait()
    parts = jnp.concatenate([plain, plain * waves[0:1, :], plain * waves[1:2, :]], axis=0)
    copies[2].wait()
    spectra = dot_split(parts, table)
    flat, with_cos, with_sin = (spectra[n * rows : (n + 1) * rows] for n in range(3))

    def later(values, steps):
        return pltpu.roll(values, rows - steps, 0)

    first = flat - with_cos
    second = later(flat + with_sin, 1)
    third = later(flat + with_cos, 2)
    fourth = later(flat - with_sin, 3)
    cos_turn, sin_turn, sign = waves[2:3, :], waves[3:4, :], waves[4:5, :]
    both = second + fourth
    diff = second - fourth
    re = (
        first[:, :BINS]
        + third[:, :BINS] * sign
        + (both[:, :BINS] * cos_turn + diff[:, BINS:] * sin_turn)
    )
    im = (
        first[:, BINS:]
        + third[:, BINS:] * sign
        + (both[:, BINS:] * cos_turn - diff[:, :BINS] * sin_turn)
    )
    amp = jnp.sqrt(re * re + im * im)
    bins = lax.broadcasted_iota(jnp.int32, (1, BINS), 1)
    total = amp
    for step in (1, 2):
        total = total + jnp.where(bins >= step, pltpu.roll(amp, step, 1), 0.0)
        total = total + jnp.where(bins < BINS - step, pltpu.roll(amp, BINS - step, 1), 0.0)
    level = jnp.sum(amp, axis=1, keepdims=True) * (1.0 / BINS)
    for copy in copies[3:7]:
        copy.wait()
    factor = 1.0 / (total / 5.0 + 0.1 * level + 1e-06)
    keep = jnp.concatenate(
        [
            jnp.broadcast_to(
                jnp.where(
                    (bins >= band_lo[k]) & (bins < jnp.where(live[k] == 1, band_hi[k], 0)), 1.0, 0.0
                ),
                (BLOCKS, BINS),
            )
            for k in range(count)
        ],
        axis=0,
    )
    factor = factor * keep
    re, im = re * factor, im * factor
    for t in range(BINS // LANES):
        white[t] = re[:, t * LANES : (t + 1) * LANES]
        white[t + BINS // LANES] = im[:, t * LANES : (t + 1) * LANES]
    for t in range(2 * BINS // LANES):
        picked = [
            white[t, pl.ds(k * BLOCKS + lax.div(offsets[k, s], QUARTER), 1), :]
            for k in range(count)
            for s in range(SEG)
        ]
        out[:, t * LANES : (t + 1) * LANES] = jnp.concatenate(picked, axis=0).astype(jnp.bfloat16)
    copies[7].wait()


def whiten(traces, offsets, band_lo, band_hi, live):
    count = traces.shape[0]
    rows = count * BLOCKS
    tables = (wave_rows(), quarter_table(), lag_table())
    return pl.pallas_call(
        whiten_kernel,
        out_shape=(
            pltpu.VMEM((count * SEG, 2 * BINS), jnp.bfloat16),
            pltpu.VMEM(tables[2].shape, jnp.bfloat16),
        ),
        in_specs=[pl.BlockSpec(memory_space=pl.ANY)] * 8,
        out_specs=(VMEM, VMEM),
        scratch_shapes=[
            pltpu.SMEM(offsets.shape, jnp.int32),
            pltpu.SMEM(band_lo.shape, jnp.int32),
            pltpu.SMEM(band_hi.shape, jnp.int32),
            pltpu.SMEM(live.shape, jnp.int32),
            pltpu.VMEM(traces.shape, jnp.float32),
            pltpu.VMEM(tables[0].shape, jnp.float32),
            pltpu.VMEM(tables[1].shape, jnp.bfloat16),
            pltpu.VMEM((rows, QUARTER), jnp.float32),
            pltpu.VMEM((2 * BINS // LANES, rows, LANES), jnp.float32),
            pltpu.SemaphoreType.DMA((8,)),
        ],
        name="whiten",
    )(offsets, band_lo, band_hi, live, traces, *(jnp.asarray(table) for table in tables))


def correlate_kernel(count, first_masks, second_masks, *refs):
    n_first, n_second = len(first_masks), len(second_masks)
    second_refs, first_refs = refs[:n_second], refs[n_second : n_first + n_second]
    table, out, left, right, cross = refs[n_first + n_second :]
    wide = count * n_second
    for n, ref in enumerate(second_refs):
        for k in range(count):
            rows = ref[k * SEG : (k + 1) * SEG, :].astype(jnp.float32)
            for t in range(2 * BINS // LANES):
                right[t, pl.ds(n * count + k, SEG, stride=wide), :] = rows[
                    :, t * LANES : (t + 1) * LANES
                ]
    at = 0
    for ref in first_refs:
        left[at : at + ref.shape[0], :] = ref[...].astype(jnp.float32)
        at += ref.shape[0]
    channels = at // SEG

    @pl.loop(0, channels, unroll=4)
    def _(i):
        there = pl.ds(pl.multiple_of(i * wide, wide), wide)
        segments = pl.ds(pl.multiple_of(i * SEG, SEG), SEG)
        for t in range(BINS // LANES):
            re = pl.ds(t * LANES, LANES)
            im = pl.ds(BINS + t * LANES, LANES)
            cross_re = jnp.zeros((wide, LANES), jnp.float32)
            cross_im = jnp.zeros((wide, LANES), jnp.float32)
            rows_re, rows_im = left[segments, re], left[segments, im]
            for s in range(SEG):
                left_re, left_im = rows_re[s : s + 1, :], rows_im[s : s + 1, :]
                right_re = right[t, s * wide : (s + 1) * wide, :]
                right_im = right[t + BINS // LANES, s * wide : (s + 1) * wide, :]
                cross_re = cross_re + (left_re * right_re + left_im * right_im)
                cross_im = cross_im + (left_im * right_re - left_re * right_im)
            cross[there, re] = cross_re
            cross[there, im] = cross_im

    row_index, col_index = lax.axis_index("row"), lax.axis_index("col")
    at = 0
    whole = dot_split(cross[...], table).astype(jnp.bfloat16)
    for masks in first_masks:
        for mask in masks:
            size = count * wide
            corr = whole[at : at + size]
            at += size
            for k in range(count):
                for n, row_mask in enumerate(second_masks):
                    start = k * wide + n * count
                    out[(col_index ^ mask) * count + k, 0, row_index ^ row_mask] = corr[
                        start : start + count, :
                    ]


def correlate(count, n_row, n_col, first, second, lags):
    first_masks = tuple(tuple(masks) for masks, _ in first)
    second_masks = tuple(mask for masks, _ in second for mask in masks)
    channels, wide = count * n_col, count * n_row
    return pl.pallas_call(
        functools.partial(correlate_kernel, count, first_masks, second_masks),
        out_shape=jax.ShapeDtypeStruct((channels, 1, n_row, count, LAGS), jnp.bfloat16),
        in_specs=[VMEM] * (len(first) + len(second) + 1),
        out_specs=VMEM,
        scratch_shapes=[
            pltpu.VMEM((channels * SEG, 2 * BINS), jnp.float32),
            pltpu.VMEM((2 * BINS // LANES, wide * SEG, LANES), jnp.float32),
            pltpu.VMEM((channels * wide, 2 * BINS), jnp.float32),
        ],
        name="correlate",
    )(*(in_vmem(a) for _, a in second + first), in_vmem(lags))


def swap(block, axis, mask):
    return lax.ppermute(block, axis, [(i, i ^ mask) for i in range(lax.axis_size(axis))])


def body(traces, offsets, band_lo, band_hi, live):
    count = traces.shape[0]
    n_row, n_col = lax.axis_size("row"), lax.axis_size("col")
    white, lags = whiten(traces, offsets, band_lo, band_hi, live)
    second = [([0], white)]
    bit = n_row // 2
    while bit:
        second += [([masks[0] ^ bit], swap(block, "row", bit)) for masks, block in second]
        bit //= 2
    held, masks = white, [0]
    bit = n_col // 2
    while bit > 2:
        across = bit + bit // 2
        held = jnp.concatenate([held, swap(held, "col", across)], axis=0)
        masks = masks + [mask ^ across for mask in masks]
        bit //= 2
    first = [(masks, held)]
    for step in (2, 1, 3):
        if step < n_col:
            first.append(([mask ^ step for mask in masks], swap(held, "col", step)))
    return correlate(count, n_row, n_col, first, second, lags)


def solution(mesh):
    in_specs = (
        P(("row", "col"), None),
        P(("row", "col"), None),
        P(("row", "col")),
        P(("row", "col")),
        P(("row", "col")),
    )
    out_specs = P("row", "col", None, None, None)
    return jax.shard_map(body, mesh=mesh, in_specs=in_specs, out_specs=out_specs, check_vma=False)
```

```python
import functools
import math

import jax
import jax.numpy as jnp
import numpy as np
from jax import lax
from jax.experimental import pallas as pl
from jax.experimental.pallas import tpu as pltpu
from jax.sharding import PartitionSpec as P

SEG = 8
SAMPLES = 1024
BINS = 256
LAGS = 512
QUARTER = SAMPLES // 4
EIGHTH = SAMPLES // 8
LANES = 128
VMEM = pl.BlockSpec(memory_space=pltpu.VMEM)
SMEM = pl.BlockSpec(memory_space=pltpu.SMEM)


def split(values):
    high = values.astype(jnp.bfloat16)
    return high, (values - high.astype(jnp.float32)).astype(jnp.bfloat16)


def split_table(table):
    high = table.astype(jnp.bfloat16)
    return np.stack([high, (table - high.astype(np.float64)).astype(jnp.bfloat16)])


def eighth_table():
    times = np.arange(EIGHTH)
    freqs = np.arange(BINS) + 1
    phase = (times[:, None] * freqs[None, :] % SAMPLES) * (2.0 * math.pi / SAMPLES)
    return split_table(np.concatenate([np.cos(phase), -np.sin(phase)], axis=1))


def wave_rows():
    times = np.arange(SAMPLES) * (2.0 * math.pi / SAMPLES)
    freqs = np.arange(BINS) + 1
    eighth = (freqs % 8) * (math.pi / 4.0)
    cos_turn = np.array([1.0, 0.0, -1.0, 0.0])[freqs % 4]
    sin_turn = np.array([0.0, 1.0, 0.0, -1.0])[freqs % 4]
    taper = (0.5 - 0.5 * np.cos(times)).reshape(4, QUARTER)
    return np.stack([*taper, cos_turn, sin_turn, np.cos(eighth), np.sin(eighth)]).astype(np.float32)


def lag_table():
    freqs = np.arange(BINS) + 1
    shifts = np.arange(LAGS) - LAGS // 2
    phase = (freqs[:, None] * shifts[None, :] % SAMPLES) * (2.0 * math.pi / SAMPLES)
    table = np.concatenate([np.cos(phase), -np.sin(phase)], axis=0)
    return (table / math.sqrt(SEG * BINS)).astype(jnp.bfloat16)


def in_vmem(array):
    return pltpu.with_memory_space_constraint(array, pltpu.VMEM)


def dot(left, right):
    return jnp.dot(left, right, preferred_element_type=jnp.float32)


def whiten_kernel(offsets, band_lo, band_hi, live, traces, waves, table, out, quarters):
    count = traces.shape[0]
    rows = count * SEG
    for k in range(count):
        for s in range(SEG):
            start = pl.multiple_of(offsets[k, s], QUARTER)
            segment = traces[pl.ds(k, 1), pl.ds(start, SAMPLES)]
            for q in range(4):
                quarters[pl.ds(q * rows + k * SEG + s, 1), :] = segment[
                    :, q * QUARTER : (q + 1) * QUARTER
                ]
    parts = jnp.concatenate(
        [quarters[q * rows : (q + 1) * rows, :] * waves[q : q + 1, :] for q in range(4)], axis=0
    )
    high, low = split(jnp.concatenate([parts[:, :EIGHTH], parts[:, EIGHTH:]], axis=0))
    spectra = dot(
        jnp.concatenate([high, low, high], axis=1),
        jnp.concatenate([table[0], table[0], table[1]], axis=0),
    )
    cos_turn, sin_turn = waves[4:5, :], waves[5:6, :]
    sign = cos_turn * cos_turn - sin_turn * sin_turn

    def turned(n):
        quarter = [spectra[(n + q) * rows : (n + q + 1) * rows] for q in range(4)]
        re, im = [x[:, :BINS] for x in quarter], [x[:, BINS:] for x in quarter]
        return (
            (re[0] + re[2] * sign) + ((re[1] + re[3]) * cos_turn + (im[1] - im[3]) * sin_turn),
            (im[0] + im[2] * sign) + ((im[1] + im[3]) * cos_turn + (re[3] - re[1]) * sin_turn),
        )

    early_re, early_im = turned(0)
    late_re, late_im = turned(4)
    cos_eighth, sin_eighth = waves[6:7, :], waves[7:8, :]
    re = early_re + (late_re * cos_eighth + late_im * sin_eighth)
    im = early_im + (late_im * cos_eighth - late_re * sin_eighth)
    amp = jnp.sqrt(re * re + im * im)
    bins = lax.broadcasted_iota(jnp.int32, (1, BINS), 1)
    total = amp
    for step in (1, 2):
        total = total + jnp.where(bins >= step, pltpu.roll(amp, step, 1), 0.0)
        total = total + jnp.where(bins < BINS - step, pltpu.roll(amp, BINS - step, 1), 0.0)
    level = jnp.sum(amp, axis=1, keepdims=True) * (1.0 / BINS)
    factor = 1.0 / (total / 5.0 + 0.1 * level + 1e-06)
    keep = jnp.concatenate(
        [
            jnp.broadcast_to(
                jnp.where(
                    (bins >= band_lo[k]) & (bins < jnp.where(live[k] == 1, band_hi[k], 0)), 1.0, 0.0
                ),
                (SEG, BINS),
            )
            for k in range(count)
        ],
        axis=0,
    )
    factor = factor * keep
    out[:, :BINS] = (re * factor).astype(jnp.bfloat16)
    out[:, BINS:] = (im * factor).astype(jnp.bfloat16)


def whiten(traces, offsets, band_lo, band_hi, live):
    count = traces.shape[0]
    tables = (wave_rows(), eighth_table())
    return pl.pallas_call(
        whiten_kernel,
        out_shape=pltpu.VMEM((count * SEG, 2 * BINS), jnp.bfloat16),
        in_specs=[SMEM] * 4 + [VMEM] * 3,
        out_specs=VMEM,
        scratch_shapes=[pltpu.VMEM((4 * count * SEG, QUARTER), jnp.float32)],
        name="whiten",
    )(offsets, band_lo, band_hi, live, traces, *(jnp.asarray(table) for table in tables))


def cross_spectra(first_refs, left, right, cross, wide):
    at = 0
    for ref in first_refs:
        left[at : at + ref.shape[0], :] = ref[...].astype(jnp.float32)
        at += ref.shape[0]

    @pl.loop(0, left.shape[0] // SEG, unroll=4)
    def _(i):
        there = pl.ds(pl.multiple_of(i * wide, wide), wide)
        segments = pl.ds(pl.multiple_of(i * SEG, SEG), SEG)
        for t in range(BINS // LANES):
            re = pl.ds(t * LANES, LANES)
            im = pl.ds(BINS + t * LANES, LANES)
            cross_re = jnp.zeros((wide, LANES), jnp.float32)
            cross_im = jnp.zeros((wide, LANES), jnp.float32)
            rows_re, rows_im = left[segments, re], left[segments, im]
            for s in range(SEG):
                left_re, left_im = rows_re[s : s + 1, :], rows_im[s : s + 1, :]
                right_re = right[t, s * wide : (s + 1) * wide, :]
                right_im = right[t + BINS // LANES, s * wide : (s + 1) * wide, :]
                cross_re = cross_re + (left_re * right_re + left_im * right_im)
                cross_im = cross_im + (left_im * right_re - left_re * right_im)
            cross[there, re] = cross_re
            cross[there, im] = cross_im


def load_kernel(table, after, out, arrived):
    copy = pltpu.make_async_copy(table, out, arrived)
    copy.start()
    copy.wait()


def load_lags(after):
    table = lag_table()
    return pl.pallas_call(
        load_kernel,
        out_shape=pltpu.VMEM(table.shape, table.dtype),
        in_specs=[pl.BlockSpec(memory_space=pl.ANY), VMEM],
        out_specs=VMEM,
        scratch_shapes=[pltpu.SemaphoreType.DMA(())],
        name="load_lags",
    )(jnp.asarray(table), in_vmem(after))


def prepare_kernel(count, n_second, *refs):
    second_refs = refs[:n_second]
    *first_refs, right, cross, left = refs[n_second:]
    wide = count * n_second
    for n, ref in enumerate(second_refs):
        for k in range(count):
            rows = ref[k * SEG : (k + 1) * SEG, :].astype(jnp.float32)
            for t in range(2 * BINS // LANES):
                right[t, pl.ds(n * count + k, SEG, stride=wide), :] = rows[
                    :, t * LANES : (t + 1) * LANES
                ]
    cross_spectra(first_refs, left, right, cross, wide)


def prepare(count, second, first):
    wide = count * len(second)
    rows = sum(block.shape[0] for block in first)
    return pl.pallas_call(
        functools.partial(prepare_kernel, count, len(second)),
        out_shape=(
            pltpu.VMEM((2 * BINS // LANES, wide * SEG, LANES), jnp.float32),
            pltpu.VMEM((rows // SEG * wide, 2 * BINS), jnp.float32),
        ),
        in_specs=[VMEM] * (len(second) + len(first)),
        out_specs=(VMEM, VMEM),
        scratch_shapes=[pltpu.VMEM((rows, 2 * BINS), jnp.float32)],
        name="prepare",
    )(*(in_vmem(block) for block in (*second, *first)))


def correlate_kernel(count, bits, steps, row_masks, *refs):
    right, ready, table, *first_refs, out, left, cross = refs
    wide = count * len(row_masks)
    cross_spectra(first_refs, left, right, cross, wide)
    high, low = split(jnp.concatenate([ready[...], cross[...]], axis=0))
    corr = dot(
        jnp.concatenate([high, low], axis=1), jnp.concatenate([table[...], table[...]], axis=0)
    ).astype(jnp.bfloat16)
    row_index, col_index = lax.axis_index("row"), lax.axis_index("col")
    held = [col_index]
    for bit in bits:
        across = jnp.where(col_index & bit == 0, far(bit), bit)
        held += [col ^ across for col in held]
    at = 0
    for col in (col ^ step for step in steps for col in held):
        for k in range(count):
            for row_mask in row_masks:
                out[col * count + k, 0, row_index ^ row_mask] = corr[at : at + count, :]
                at += count


def correlate(count, n_row, n_col, bits, steps, row_masks, prepared, lags, first):
    channels, wide = count * n_col, count * n_row
    rows = sum(block.shape[0] for block in first)
    return pl.pallas_call(
        functools.partial(correlate_kernel, count, bits, steps, row_masks),
        out_shape=jax.ShapeDtypeStruct((channels, 1, n_row, count, LAGS), jnp.bfloat16),
        in_specs=[VMEM] * (3 + len(first)),
        out_specs=VMEM,
        scratch_shapes=[
            pltpu.VMEM((rows, 2 * BINS), jnp.float32),
            pltpu.VMEM((rows // SEG * wide, 2 * BINS), jnp.float32),
        ],
        name="correlate",
    )(*(in_vmem(block) for block in (*prepared, lags, *first)))


def swap(block, axis, mask):
    return lax.ppermute(block, axis, [(i, i ^ mask) for i in range(lax.axis_size(axis))])


def far(bit):
    return bit + bit // 2


def cross_over(block, bit):
    pairs = [(i, i ^ (far(bit) if i & bit else bit)) for i in range(lax.axis_size("col"))]
    return lax.ppermute(block, "col", pairs)


def body(traces, offsets, band_lo, band_hi, live):
    count = traces.shape[0]
    n_row, n_col = lax.axis_size("row"), lax.axis_size("col")
    white = whiten(traces, offsets, band_lo, band_hi, live)
    second, row_masks = [white], [0]
    bit = n_row // 2
    while bit:
        second += [swap(block, "row", bit) for block in second]
        row_masks += [mask ^ bit for mask in row_masks]
        bit //= 2
    held, bits = white, []
    bit = n_col // 2
    while bit > 2:
        held = jnp.concatenate([held, cross_over(held, bit)], axis=0)
        bits.append(bit)
        bit //= 2
    steps = [step for step in (3, 1, 2) if step < n_col]
    near = [swap(held, "col", step) for step in steps]
    prepared = prepare(count, second, [held, *near[:1]])
    lags = load_lags(second[1])
    return correlate(
        count, n_row, n_col, bits, [0, *steps[:1], *steps[:0:-1]], row_masks, prepared, lags, near[:0:-1]
    )


def solution(mesh):
    in_specs = (
        P(("row", "col"), None),
        P(("row", "col"), None),
        P(("row", "col")),
        P(("row", "col")),
        P(("row", "col")),
    )
    out_specs = P("row", "col", None, None, None)
    return jax.shard_map(body, mesh=mesh, in_specs=in_specs, out_specs=out_specs, check_vma=False)
```

```python
import functools
import math

import jax
import jax.numpy as jnp
import numpy as np
from jax import lax
from jax.experimental import pallas as pl
from jax.experimental.pallas import tpu as pltpu
from jax.sharding import PartitionSpec as P

SEG = 8
SAMPLES = 1024
BINS = 256
LAGS = 512
QUARTER = SAMPLES // 4
EIGHTH = SAMPLES // 8
LANES = 128
VMEM = pl.BlockSpec(memory_space=pltpu.VMEM)
SMEM = pl.BlockSpec(memory_space=pltpu.SMEM)


def split(values):
    high = values.astype(jnp.bfloat16)
    return high, (values - high.astype(jnp.float32)).astype(jnp.bfloat16)


def split_table(table):
    high = table.astype(jnp.bfloat16)
    return np.stack([high, (table - high.astype(np.float64)).astype(jnp.bfloat16)])


def eighth_table():
    times = np.arange(EIGHTH)
    freqs = np.arange(BINS) + 1
    phase = (times[:, None] * freqs[None, :] % SAMPLES) * (2.0 * math.pi / SAMPLES)
    return split_table(np.concatenate([np.cos(phase), -np.sin(phase)], axis=1))


def wave_rows():
    times = np.arange(SAMPLES) * (2.0 * math.pi / SAMPLES)
    freqs = np.arange(BINS) + 1
    eighth = (freqs % 8) * (math.pi / 4.0)
    cos_turn = np.array([1.0, 0.0, -1.0, 0.0])[freqs % 4]
    sin_turn = np.array([0.0, 1.0, 0.0, -1.0])[freqs % 4]
    taper = (0.5 - 0.5 * np.cos(times)).reshape(4, QUARTER)
    return np.stack([*taper, cos_turn, sin_turn, np.cos(eighth), np.sin(eighth)]).astype(np.float32)


def lag_table():
    freqs = np.arange(BINS) + 1
    shifts = np.arange(LAGS) - LAGS // 2
    phase = (freqs[:, None] * shifts[None, :] % SAMPLES) * (2.0 * math.pi / SAMPLES)
    table = np.concatenate([np.cos(phase), -np.sin(phase)], axis=0)
    return (table / math.sqrt(SEG * BINS)).astype(jnp.bfloat16)


def in_vmem(array):
    return pltpu.with_memory_space_constraint(array, pltpu.VMEM)


def dot(left, right):
    return jnp.dot(left, right, preferred_element_type=jnp.float32)


def whiten_kernel(offsets, band_lo, band_hi, live, traces, waves, table, out, quarters):
    count = traces.shape[0]
    rows = count * SEG
    for k in range(count):
        for s in range(SEG):
            start = pl.multiple_of(offsets[k, s], QUARTER)
            segment = traces[pl.ds(k, 1), pl.ds(start, SAMPLES)]
            for q in range(4):
                quarters[pl.ds(q * rows + k * SEG + s, 1), :] = segment[
                    :, q * QUARTER : (q + 1) * QUARTER
                ]
    parts = jnp.concatenate(
        [quarters[q * rows : (q + 1) * rows, :] * waves[q : q + 1, :] for q in range(4)], axis=0
    )
    high, low = split(jnp.concatenate([parts[:, :EIGHTH], parts[:, EIGHTH:]], axis=0))
    spectra = dot(
        jnp.concatenate([high, low, high], axis=1),
        jnp.concatenate([table[0], table[0], table[1]], axis=0),
    )
    cos_turn, sin_turn = waves[4:5, :], waves[5:6, :]
    sign = cos_turn * cos_turn - sin_turn * sin_turn

    def turned(n):
        quarter = [spectra[(n + q) * rows : (n + q + 1) * rows] for q in range(4)]
        re, im = [x[:, :BINS] for x in quarter], [x[:, BINS:] for x in quarter]
        return (
            (re[0] + re[2] * sign) + ((re[1] + re[3]) * cos_turn + (im[1] - im[3]) * sin_turn),
            (im[0] + im[2] * sign) + ((im[1] + im[3]) * cos_turn + (re[3] - re[1]) * sin_turn),
        )

    early_re, early_im = turned(0)
    late_re, late_im = turned(4)
    cos_eighth, sin_eighth = waves[6:7, :], waves[7:8, :]
    re = early_re + (late_re * cos_eighth + late_im * sin_eighth)
    im = early_im + (late_im * cos_eighth - late_re * sin_eighth)
    amp = jnp.sqrt(re * re + im * im)
    bins = lax.broadcasted_iota(jnp.int32, (1, BINS), 1)
    total = amp
    for step in (1, 2):
        total = total + jnp.where(bins >= step, pltpu.roll(amp, step, 1), 0.0)
        total = total + jnp.where(bins < BINS - step, pltpu.roll(amp, BINS - step, 1), 0.0)
    level = jnp.sum(amp, axis=1, keepdims=True) * (1.0 / BINS)
    factor = 1.0 / (total / 5.0 + 0.1 * level + 1e-06)
    keep = jnp.concatenate(
        [
            jnp.broadcast_to(
                jnp.where(
                    (bins >= band_lo[k]) & (bins < jnp.where(live[k] == 1, band_hi[k], 0)), 1.0, 0.0
                ),
                (SEG, BINS),
            )
            for k in range(count)
        ],
        axis=0,
    )
    factor = factor * keep
    out[:, :BINS] = (re * factor).astype(jnp.bfloat16)
    out[:, BINS:] = (im * factor).astype(jnp.bfloat16)


def whiten(traces, offsets, band_lo, band_hi, live):
    count = traces.shape[0]
    tables = (wave_rows(), eighth_table())
    return pl.pallas_call(
        whiten_kernel,
        out_shape=pltpu.VMEM((count * SEG, 2 * BINS), jnp.bfloat16),
        in_specs=[SMEM] * 4 + [VMEM] * 3,
        out_specs=VMEM,
        scratch_shapes=[pltpu.VMEM((4 * count * SEG, QUARTER), jnp.float32)],
        name="whiten",
    )(offsets, band_lo, band_hi, live, traces, *(jnp.asarray(table) for table in tables))


def cross_spectra(first_refs, left, right, cross, wide):
    at = 0
    for ref in first_refs:
        left[at : at + ref.shape[0], :] = ref[...].astype(jnp.float32)
        at += ref.shape[0]

    @pl.loop(0, left.shape[0] // SEG, unroll=4)
    def _(i):
        there = pl.ds(pl.multiple_of(i * wide, wide), wide)
        segments = pl.ds(pl.multiple_of(i * SEG, SEG), SEG)
        for t in range(BINS // LANES):
            re = pl.ds(t * LANES, LANES)
            im = pl.ds(BINS + t * LANES, LANES)
            cross_re = jnp.zeros((wide, LANES), jnp.float32)
            cross_im = jnp.zeros((wide, LANES), jnp.float32)
            rows_re, rows_im = left[segments, re], left[segments, im]
            for s in range(SEG):
                left_re, left_im = rows_re[s : s + 1, :], rows_im[s : s + 1, :]
                right_re = right[t, s * wide : (s + 1) * wide, :]
                right_im = right[t + BINS // LANES, s * wide : (s + 1) * wide, :]
                cross_re = cross_re + (left_re * right_re + left_im * right_im)
                cross_im = cross_im + (left_im * right_re - left_re * right_im)
            cross[there, re] = cross_re
            cross[there, im] = cross_im


def load_kernel(table, after, out, arrived):
    copy = pltpu.make_async_copy(table, out, arrived)
    copy.start()
    copy.wait()


def load_lags(after):
    table = lag_table()
    return pl.pallas_call(
        load_kernel,
        out_shape=pltpu.VMEM(table.shape, table.dtype),
        in_specs=[pl.BlockSpec(memory_space=pl.ANY), VMEM],
        out_specs=VMEM,
        scratch_shapes=[pltpu.SemaphoreType.DMA(())],
        name="load_lags",
        cost_estimate=pl.CostEstimate(flops=1000000000, bytes_accessed=10000000, transcendentals=0),
    )(jnp.asarray(table), in_vmem(after))


def correlations(cross, table, out, row_masks):
    count = out.shape[3]
    high, low = split(cross[...])
    both = dot(jnp.concatenate([high, low], axis=0), table[...])
    corr = (both[: high.shape[0]] + both[high.shape[0] :]).astype(jnp.bfloat16)
    row_index = lax.axis_index("row")
    at = 0
    for i in range(out.shape[0]):
        for row_mask in row_masks:
            out[i, 0, row_index ^ row_mask] = corr[at : at + count, :]
            at += count


def prepare_kernel(count, row_masks, *refs):
    n_second = len(row_masks)
    second_refs = refs[:n_second]
    table, *first_refs, right, ready, left, cross = refs[n_second:]
    wide = count * n_second
    for n, ref in enumerate(second_refs):
        for k in range(count):
            rows = ref[k * SEG : (k + 1) * SEG, :].astype(jnp.float32)
            for t in range(2 * BINS // LANES):
                right[t, pl.ds(n * count + k, SEG, stride=wide), :] = rows[
                    :, t * LANES : (t + 1) * LANES
                ]
    cross_spectra(first_refs, left, right, cross, wide)
    correlations(cross, table, ready, row_masks)


def prepare(count, row_masks, second, lags, first):
    n_row = len(second)
    rows = sum(block.shape[0] for block in first)
    return pl.pallas_call(
        functools.partial(prepare_kernel, count, row_masks),
        out_shape=(
            pltpu.VMEM((2 * BINS // LANES, count * n_row * SEG, LANES), jnp.float32),
            pltpu.VMEM((rows // SEG, 1, n_row, count, LAGS), jnp.bfloat16),
        ),
        in_specs=[VMEM] * (len(second) + 1 + len(first)),
        out_specs=(VMEM, VMEM),
        scratch_shapes=[
            pltpu.VMEM((rows, 2 * BINS), jnp.float32),
            pltpu.VMEM((rows // SEG * count * n_row, 2 * BINS), jnp.float32),
        ],
        name="prepare",
    )(*(in_vmem(block) for block in (*second, lags, *first)))


def stage_kernel(row_masks, right, table, *refs):
    *first_refs, ready, left, cross = refs
    cross_spectra(first_refs, left, right, cross, right.shape[1] // SEG)
    correlations(cross, table, ready, row_masks)


def stage(count, row_masks, right, lags, first):
    n_row = len(row_masks)
    rows = sum(block.shape[0] for block in first)
    return pl.pallas_call(
        functools.partial(stage_kernel, row_masks),
        out_shape=pltpu.VMEM((rows // SEG, 1, n_row, count, LAGS), jnp.bfloat16),
        in_specs=[VMEM] * (2 + len(first)),
        out_specs=VMEM,
        scratch_shapes=[
            pltpu.VMEM((rows, 2 * BINS), jnp.float32),
            pltpu.VMEM((rows // SEG * count * n_row, 2 * BINS), jnp.float32),
        ],
        name="stage",
    )(*(in_vmem(block) for block in (right, lags, *first)))


def correlate_kernel(count, n_ready, bits, steps, row_masks, *refs):
    ready = refs[:n_ready]
    right, table, *first_refs, out, left, cross, last, sent = refs[n_ready:]
    col_index = lax.axis_index("col")
    held = [col_index]
    for bit in bits:
        across = jnp.where(col_index & bit == 0, far(bit), bit)
        held += [col ^ across for col in held]
    cols = [col ^ step for step in steps for col in held]
    blocks = [
        ref.at[pl.ds(at, count)] for ref in (*ready, last) for at in range(0, ref.shape[0], count)
    ]
    copies = [
        pltpu.make_async_copy(block, out.at[pl.ds(col * count, count)], sent.at[n])
        for n, (block, col) in enumerate(zip(blocks, cols, strict=True))
    ]
    early = len(blocks) - last.shape[0] // count
    for copy in copies[:early]:
        copy.start()
    cross_spectra(first_refs, left, right, cross, count * len(row_masks))
    correlations(cross, table, last, row_masks)
    for copy in copies[early:]:
        copy.start()
    for copy in copies:
        copy.wait()


def correlate(count, n_row, n_col, bits, steps, row_masks, ready, right, lags, first):
    channels, wide = count * n_col, count * n_row
    rows = sum(block.shape[0] for block in first)
    return pl.pallas_call(
        functools.partial(correlate_kernel, count, len(ready), bits, steps, row_masks),
        out_shape=jax.ShapeDtypeStruct((channels, 1, n_row, count, LAGS), jnp.bfloat16),
        in_specs=[VMEM] * (len(ready) + 2 + len(first)),
        out_specs=pl.BlockSpec(memory_space=pl.ANY),
        scratch_shapes=[
            pltpu.VMEM((rows, 2 * BINS), jnp.float32),
            pltpu.VMEM((rows // SEG * wide, 2 * BINS), jnp.float32),
            pltpu.VMEM((rows // SEG, 1, n_row, count, LAGS), jnp.bfloat16),
            pltpu.SemaphoreType.DMA((n_col,)),
        ],
        name="correlate",
    )(*(in_vmem(block) for block in (*ready, right, lags, *first)))


def swap(block, axis, mask):
    return lax.ppermute(block, axis, [(i, i ^ mask) for i in range(lax.axis_size(axis))])


def far(bit):
    return bit + bit // 2


def cross_over(block, bit):
    pairs = [(i, i ^ (far(bit) if i & bit else bit)) for i in range(lax.axis_size("col"))]
    return lax.ppermute(block, "col", pairs)


def body(traces, offsets, band_lo, band_hi, live):
    count = traces.shape[0]
    n_row, n_col = lax.axis_size("row"), lax.axis_size("col")
    white = whiten(traces, offsets, band_lo, band_hi, live)
    second, row_masks = [white], [0]
    bit = n_row // 2
    while bit:
        second += [swap(block, "row", bit) for block in second]
        row_masks += [mask ^ bit for mask in row_masks]
        bit //= 2
    held, bits = white, []
    bit = n_col // 2
    while bit > 2:
        held = jnp.concatenate([held, cross_over(held, bit)], axis=0)
        bits.append(bit)
        bit //= 2
    steps = [step for step in (3, 1, 2) if step < n_col]
    near = [swap(held, "col", step) for step in steps]
    lags = load_lags(second[2])
    right, *ready = prepare(count, row_masks, second, lags, [held, *near[:-2]])
    ready += [stage(count, row_masks, right, lags, [block]) for block in near[-2:-1]]
    return correlate(
        count, n_row, n_col, bits, [0, *steps], row_masks, ready, right, lags, near[-1:]
    )


def solution(mesh):
    in_specs = (
        P(("row", "col"), None),
        P(("row", "col"), None),
        P(("row", "col")),
        P(("row", "col")),
        P(("row", "col")),
    )
    out_specs = P("row", "col", None, None, None)
    return jax.shard_map(body, mesh=mesh, in_specs=in_specs, out_specs=out_specs, check_vma=False)
```

```python
import functools
import math

import jax
import jax.numpy as jnp
import numpy as np
from jax import lax
from jax.experimental import pallas as pl
from jax.experimental.pallas import tpu as pltpu
from jax.sharding import PartitionSpec as P

SEG = 8
SAMPLES = 1024
BINS = 256
LAGS = 512
QUARTER = SAMPLES // 4
EIGHTH = SAMPLES // 8
LANES = 128
VMEM = pl.BlockSpec(memory_space=pltpu.VMEM)
SMEM = pl.BlockSpec(memory_space=pltpu.SMEM)


def split(values):
    high = values.astype(jnp.bfloat16)
    return high, (values - high.astype(jnp.float32)).astype(jnp.bfloat16)


def split_table(table):
    high = table.astype(jnp.bfloat16)
    return np.stack([high, (table - high.astype(np.float64)).astype(jnp.bfloat16)])


def eighth_table():
    times = np.arange(EIGHTH)
    freqs = np.arange(BINS) + 1
    phase = (times[:, None] * freqs[None, :] % SAMPLES) * (2.0 * math.pi / SAMPLES)
    return split_table(np.concatenate([np.cos(phase), -np.sin(phase)], axis=1))


def wave_rows():
    times = np.arange(SAMPLES) * (2.0 * math.pi / SAMPLES)
    freqs = np.arange(BINS) + 1
    eighth = (freqs % 8) * (math.pi / 4.0)
    cos_turn = np.array([1.0, 0.0, -1.0, 0.0])[freqs % 4]
    sin_turn = np.array([0.0, 1.0, 0.0, -1.0])[freqs % 4]
    taper = (0.5 - 0.5 * np.cos(times)).reshape(4, QUARTER)
    return np.stack([*taper, cos_turn, sin_turn, np.cos(eighth), np.sin(eighth)]).astype(np.float32)


def lag_table():
    freqs = np.arange(BINS) + 1
    shifts = np.arange(LAGS) - LAGS // 2
    phase = (freqs[:, None] * shifts[None, :] % SAMPLES) * (2.0 * math.pi / SAMPLES)
    table = np.concatenate([np.cos(phase), -np.sin(phase)], axis=0)
    return (table / math.sqrt(SEG * BINS)).astype(jnp.bfloat16)


def in_vmem(array):
    return pltpu.with_memory_space_constraint(array, pltpu.VMEM)


def dot(left, right):
    return jnp.dot(left, right, preferred_element_type=jnp.float32)


def whiten_kernel(offsets, band_lo, band_hi, live, traces, waves, table, out, quarters):
    count = traces.shape[0]
    rows = count * SEG
    for k in range(count):
        for s in range(SEG):
            start = pl.multiple_of(offsets[k, s], QUARTER)
            segment = traces[pl.ds(k, 1), pl.ds(start, SAMPLES)]
            for q in range(4):
                quarters[pl.ds(q * rows + k * SEG + s, 1), :] = segment[
                    :, q * QUARTER : (q + 1) * QUARTER
                ]
    parts = jnp.concatenate(
        [quarters[q * rows : (q + 1) * rows, :] * waves[q : q + 1, :] for q in range(4)], axis=0
    )
    high, low = split(jnp.concatenate([parts[:, :EIGHTH], parts[:, EIGHTH:]], axis=0))
    spectra = dot(
        jnp.concatenate([high, low, high], axis=1),
        jnp.concatenate([table[0], table[0], table[1]], axis=0),
    )
    cos_turn, sin_turn = waves[4:5, :], waves[5:6, :]
    sign = cos_turn * cos_turn - sin_turn * sin_turn

    def turned(n):
        quarter = [spectra[(n + q) * rows : (n + q + 1) * rows] for q in range(4)]
        re, im = [x[:, :BINS] for x in quarter], [x[:, BINS:] for x in quarter]
        return (
            (re[0] + re[2] * sign) + ((re[1] + re[3]) * cos_turn + (im[1] - im[3]) * sin_turn),
            (im[0] + im[2] * sign) + ((im[1] + im[3]) * cos_turn + (re[3] - re[1]) * sin_turn),
        )

    early_re, early_im = turned(0)
    late_re, late_im = turned(4)
    cos_eighth, sin_eighth = waves[6:7, :], waves[7:8, :]
    re = early_re + (late_re * cos_eighth + late_im * sin_eighth)
    im = early_im + (late_im * cos_eighth - late_re * sin_eighth)
    amp = jnp.sqrt(re * re + im * im)
    bins = lax.broadcasted_iota(jnp.int32, (1, BINS), 1)
    total = amp
    for step in (1, 2):
        total = total + jnp.where(bins >= step, pltpu.roll(amp, step, 1), 0.0)
        total = total + jnp.where(bins < BINS - step, pltpu.roll(amp, BINS - step, 1), 0.0)
    level = jnp.sum(amp, axis=1, keepdims=True) * (1.0 / BINS)
    factor = 1.0 / (total / 5.0 + 0.1 * level + 1e-06)
    keep = jnp.concatenate(
        [
            jnp.broadcast_to(
                jnp.where(
                    (bins >= band_lo[k]) & (bins < jnp.where(live[k] == 1, band_hi[k], 0)), 1.0, 0.0
                ),
                (SEG, BINS),
            )
            for k in range(count)
        ],
        axis=0,
    )
    factor = factor * keep
    out[:, :BINS] = (re * factor).astype(jnp.bfloat16)
    out[:, BINS:] = (im * factor).astype(jnp.bfloat16)


def whiten(traces, offsets, band_lo, band_hi, live):
    count = traces.shape[0]
    tables = (wave_rows(), eighth_table())
    return pl.pallas_call(
        whiten_kernel,
        out_shape=pltpu.VMEM((count * SEG, 2 * BINS), jnp.bfloat16),
        in_specs=[SMEM] * 4 + [VMEM] * 3,
        out_specs=VMEM,
        scratch_shapes=[pltpu.VMEM((4 * count * SEG, QUARTER), jnp.float32)],
        name="whiten",
    )(offsets, band_lo, band_hi, live, traces, *(jnp.asarray(table) for table in tables))


def cross_spectra(first_refs, left, right, cross, wide):
    at = 0
    for ref in first_refs:
        left[at : at + ref.shape[0], :] = ref[...].astype(jnp.float32)
        at += ref.shape[0]

    @pl.loop(0, left.shape[0] // SEG, unroll=4)
    def _(i):
        there = pl.ds(pl.multiple_of(i * wide, wide), wide)
        segments = pl.ds(pl.multiple_of(i * SEG, SEG), SEG)
        for t in range(BINS // LANES):
            re = pl.ds(t * LANES, LANES)
            im = pl.ds(BINS + t * LANES, LANES)
            cross_re = jnp.zeros((wide, LANES), jnp.float32)
            cross_im = jnp.zeros((wide, LANES), jnp.float32)
            rows_re, rows_im = left[segments, re], left[segments, im]
            for s in range(SEG):
                left_re, left_im = rows_re[s : s + 1, :], rows_im[s : s + 1, :]
                right_re = right[t, s * wide : (s + 1) * wide, :]
                right_im = right[t + BINS // LANES, s * wide : (s + 1) * wide, :]
                cross_re = cross_re + (left_re * right_re + left_im * right_im)
                cross_im = cross_im + (left_im * right_re - left_re * right_im)
            cross[there, re] = cross_re
            cross[there, im] = cross_im


def join_kernel(own, other, out):
    out[: own.shape[0], :] = own[...]
    out[own.shape[0] :, :] = other[...]


def join(own, other, cost=10**6):
    return pl.pallas_call(
        join_kernel,
        out_shape=pltpu.VMEM((own.shape[0] + other.shape[0], own.shape[1]), own.dtype),
        in_specs=[VMEM] * 2,
        out_specs=VMEM,
        cost_estimate=pl.CostEstimate(flops=cost, bytes_accessed=cost // 100, transcendentals=0),
        name="join",
    )(in_vmem(own), in_vmem(other))


def correlations(cross, table, out, row_masks):
    count = out.shape[3]
    high, low = split(cross[...])
    both = dot(jnp.concatenate([high, low], axis=0), table[...])
    corr = (both[: high.shape[0]] + both[high.shape[0] :]).astype(jnp.bfloat16)
    row_index = lax.axis_index("row")
    at = 0
    for i in range(out.shape[0]):
        for row_mask in row_masks:
            out[i, 0, row_index ^ row_mask] = corr[at : at + count, :]
            at += count


def prepare_kernel(count, n_second, row_masks, *refs):
    second_refs = refs[:n_second]
    table, *first_refs, right, ready, left, cross = refs[n_second:]
    wide = count * len(row_masks)
    n = 0
    for ref in second_refs:
        for at in range(0, ref.shape[0], SEG):
            rows = ref[at : at + SEG, :].astype(jnp.float32)
            for t in range(2 * BINS // LANES):
                right[t, pl.ds(n, SEG, stride=wide), :] = rows[:, t * LANES : (t + 1) * LANES]
            n += 1
    cross_spectra(first_refs, left, right, cross, wide)
    correlations(cross, table, ready, row_masks)


def prepare(count, row_masks, second, lags, first):
    n_row = len(row_masks)
    rows = sum(block.shape[0] for block in first)
    return pl.pallas_call(
        functools.partial(prepare_kernel, count, len(second), row_masks),
        out_shape=(
            pltpu.VMEM((2 * BINS // LANES, count * n_row * SEG, LANES), jnp.float32),
            pltpu.VMEM((rows // SEG, 1, n_row, count, LAGS), jnp.bfloat16),
        ),
        in_specs=[VMEM] * (len(second) + 1 + len(first)),
        out_specs=(VMEM, VMEM),
        scratch_shapes=[
            pltpu.VMEM((rows, 2 * BINS), jnp.float32),
            pltpu.VMEM((rows // SEG * count * n_row, 2 * BINS), jnp.float32),
        ],
        name="prepare",
    )(*(in_vmem(block) for block in (*second, lags, *first)))


def stage_kernel(row_masks, right, table, *refs):
    *first_refs, ready, left, cross = refs
    cross_spectra(first_refs, left, right, cross, right.shape[1] // SEG)
    correlations(cross, table, ready, row_masks)


def stage(count, row_masks, right, lags, first):
    n_row = len(row_masks)
    rows = sum(block.shape[0] for block in first)
    return pl.pallas_call(
        functools.partial(stage_kernel, row_masks),
        out_shape=pltpu.VMEM((rows // SEG, 1, n_row, count, LAGS), jnp.bfloat16),
        in_specs=[VMEM] * (2 + len(first)),
        out_specs=VMEM,
        scratch_shapes=[
            pltpu.VMEM((rows, 2 * BINS), jnp.float32),
            pltpu.VMEM((rows // SEG * count * n_row, 2 * BINS), jnp.float32),
        ],
        name="stage",
    )(*(in_vmem(block) for block in (right, lags, *first)))


def correlate_kernel(count, n_ready, moves, bits, row_masks, *refs):
    ready = refs[:n_ready]
    right, table, *first_refs, out, left, cross, last, sent = refs[n_ready:]
    col_index = lax.axis_index("col")
    cols = [at for source in sources(col_index, moves) for at in held_at(source, moves, bits)]
    blocks = [
        ref.at[pl.ds(at, count)] for ref in (*ready, last) for at in range(0, ref.shape[0], count)
    ]
    copies = [
        pltpu.make_async_copy(block, out.at[pl.ds(col * count, count)], sent.at[n])
        for n, (block, col) in enumerate(zip(blocks, cols, strict=True))
    ]
    early = len(blocks) - last.shape[0] // count
    for copy in copies[:early]:
        copy.start()
    cross_spectra(first_refs, left, right, cross, count * len(row_masks))
    correlations(cross, table, last, row_masks)
    for copy in copies[early:]:
        copy.start()
    for copy in copies:
        copy.wait()


def correlate(count, n_row, n_col, moves, bits, row_masks, ready, right, lags, first):
    channels, wide = count * n_col, count * n_row
    rows = sum(block.shape[0] for block in first)
    return pl.pallas_call(
        functools.partial(correlate_kernel, count, len(ready), moves, bits, row_masks),
        out_shape=jax.ShapeDtypeStruct((channels, 1, n_row, count, LAGS), jnp.bfloat16),
        in_specs=[VMEM] * (len(ready) + 2 + len(first)),
        out_specs=pl.BlockSpec(memory_space=pl.ANY),
        scratch_shapes=[
            pltpu.VMEM((rows, 2 * BINS), jnp.float32),
            pltpu.VMEM((rows // SEG * wide, 2 * BINS), jnp.float32),
            pltpu.VMEM((rows // SEG, 1, n_row, count, LAGS), jnp.bfloat16),
            pltpu.SemaphoreType.DMA((n_col,)),
        ],
        name="correlate",
    )(*(in_vmem(block) for block in (*ready, right, lags, *first)))


def swap(block, axis, mask):
    return lax.ppermute(block, axis, [(i, i ^ mask) for i in range(lax.axis_size(axis))])


def moves_of(n_col):
    if n_col >= 8:
        return ((4, 1), (3, 6), (1, 4), (2, 2))
    return ((0, 0), *((step, step) for step in (3, 1, 2) if step < n_col))


def move(block, masks):
    pairs = [(i, i ^ masks[i // 2 % 2]) for i in range(lax.axis_size("col"))]
    return lax.ppermute(block, "col", pairs)


def sent_from(col, masks):
    clear, set_ = masks if clear_stays(masks) else masks[::-1]
    return col ^ jnp.where(col & 2 == 0, clear, set_)


def clear_stays(masks):
    return masks[0] & 2 == 0


def sources(col, moves):
    return [col] + [sent_from(col, masks) for masks in moves[1:]]


def held_at(col, moves, bits):
    held = [col]
    for bit in bits:
        held += [at ^ bit for at in held]
    if moves[0] != (0, 0):
        held += [at ^ sent_from(col, moves[0]) ^ col for at in held]
    return held


def body(traces, offsets, band_lo, band_hi, live):
    count = traces.shape[0]
    n_row, n_col = lax.axis_size("row"), lax.axis_size("col")
    white = whiten(traces, offsets, band_lo, band_hi, live)
    second, row_masks = [white], [0]
    bit = 1
    while bit < n_row:
        mine = second[0] if len(second) == 1 else join(*second)
        second = [mine, swap(mine, "row", bit)]
        row_masks += [mask ^ bit for mask in row_masks]
        bit *= 2
    held, bits = white, []
    bit = n_col // 2
    while bit > 4:
        held = join(held, swap(held, "col", bit))
        bits.append(bit)
        bit //= 2
    moves = moves_of(n_col)
    if moves[0] != (0, 0):
        held = join(held, move(held, moves[0]), 10**9)
    near = [move(held, masks) for masks in moves[1:]]
    lags = jnp.asarray(lag_table())
    right, *ready = prepare(count, row_masks, second, lags, [held])
    if len(near) > 1:
        ready += [stage(count, row_masks, right, lags, near[-2::-1])]
    order = (moves[0], *moves[-2:0:-1], moves[-1])
    return correlate(count, n_row, n_col, order, bits, row_masks, ready, right, lags, near[-1:])


def solution(mesh):
    in_specs = (
        P(("row", "col"), None),
        P(("row", "col"), None),
        P(("row", "col")),
        P(("row", "col")),
        P(("row", "col")),
    )
    out_specs = P("row", "col", None, None, None)
    return jax.shard_map(body, mesh=mesh, in_specs=in_specs, out_specs=out_specs, check_vma=False)
```

```python
import functools
import math

import jax
import jax.numpy as jnp
import numpy as np
from jax import lax
from jax.experimental import pallas as pl
from jax.experimental.pallas import tpu as pltpu
from jax.sharding import PartitionSpec as P

SEG = 8
SAMPLES = 1024
BINS = 256
LAGS = 512
QUARTER = SAMPLES // 4
EIGHTH = SAMPLES // 8
LANES = 128
GROUP = 8
FAR = 6
STEPS = (3, 1, 2)
VMEM = pl.BlockSpec(memory_space=pltpu.VMEM)
SMEM = pl.BlockSpec(memory_space=pltpu.SMEM)


def split(values):
    high = values.astype(jnp.bfloat16)
    return high, (values - high.astype(jnp.float32)).astype(jnp.bfloat16)


def split_table(table):
    high = table.astype(jnp.bfloat16)
    return np.stack([high, (table - high.astype(np.float64)).astype(jnp.bfloat16)])


def eighth_table():
    times = np.arange(EIGHTH)
    freqs = np.arange(BINS) + 1
    phase = (times[:, None] * freqs[None, :] % SAMPLES) * (2.0 * math.pi / SAMPLES)
    return split_table(np.concatenate([np.cos(phase), -np.sin(phase)], axis=1))


def wave_rows():
    times = np.arange(SAMPLES) * (2.0 * math.pi / SAMPLES)
    freqs = np.arange(BINS) + 1
    eighth = (freqs % 8) * (math.pi / 4.0)
    cos_turn = np.array([1.0, 0.0, -1.0, 0.0])[freqs % 4]
    sin_turn = np.array([0.0, 1.0, 0.0, -1.0])[freqs % 4]
    taper = (0.5 - 0.5 * np.cos(times)).reshape(4, QUARTER)
    return np.stack([*taper, cos_turn, sin_turn, np.cos(eighth), np.sin(eighth)]).astype(np.float32)


def lag_table():
    freqs = np.arange(BINS) + 1
    shifts = np.arange(LAGS) - LAGS // 2
    phase = (freqs[:, None] * shifts[None, :] % SAMPLES) * (2.0 * math.pi / SAMPLES)
    table = np.concatenate([np.cos(phase), -np.sin(phase)], axis=0)
    return (table / math.sqrt(SEG * BINS)).astype(jnp.bfloat16)


def in_vmem(array):
    return pltpu.with_memory_space_constraint(array, pltpu.VMEM)


def dot(left, right):
    return jnp.dot(left, right, preferred_element_type=jnp.float32)


def whiten_kernel(offsets, band_lo, band_hi, live, traces, waves, table, out, quarters):
    count = traces.shape[0]
    rows = count * SEG
    for k in range(count):
        for s in range(SEG):
            start = pl.multiple_of(offsets[k, s], QUARTER)
            segment = traces[pl.ds(k, 1), pl.ds(start, SAMPLES)]
            for q in range(4):
                quarters[pl.ds(q * rows + k * SEG + s, 1), :] = segment[
                    :, q * QUARTER : (q + 1) * QUARTER
                ]
    parts = jnp.concatenate(
        [quarters[q * rows : (q + 1) * rows, :] * waves[q : q + 1, :] for q in range(4)], axis=0
    )
    high, low = split(jnp.concatenate([parts[:, :EIGHTH], parts[:, EIGHTH:]], axis=0))
    spectra = dot(
        jnp.concatenate([high, low, high], axis=1),
        jnp.concatenate([table[0], table[0], table[1]], axis=0),
    )
    cos_turn, sin_turn = waves[4:5, :], waves[5:6, :]
    sign = cos_turn * cos_turn - sin_turn * sin_turn

    def turned(n):
        quarter = [spectra[(n + q) * rows : (n + q + 1) * rows] for q in range(4)]
        re, im = [x[:, :BINS] for x in quarter], [x[:, BINS:] for x in quarter]
        return (
            (re[0] + re[2] * sign) + ((re[1] + re[3]) * cos_turn + (im[1] - im[3]) * sin_turn),
            (im[0] + im[2] * sign) + ((im[1] + im[3]) * cos_turn + (re[3] - re[1]) * sin_turn),
        )

    early_re, early_im = turned(0)
    late_re, late_im = turned(4)
    cos_eighth, sin_eighth = waves[6:7, :], waves[7:8, :]
    re = early_re + (late_re * cos_eighth + late_im * sin_eighth)
    im = early_im + (late_im * cos_eighth - late_re * sin_eighth)
    amp = jnp.sqrt(re * re + im * im)
    bins = lax.broadcasted_iota(jnp.int32, (1, BINS), 1)
    total = amp
    for step in (1, 2):
        total = total + jnp.where(bins >= step, pltpu.roll(amp, step, 1), 0.0)
        total = total + jnp.where(bins < BINS - step, pltpu.roll(amp, BINS - step, 1), 0.0)
    level = jnp.sum(amp, axis=1, keepdims=True) * (1.0 / BINS)
    factor = 1.0 / (total / 5.0 + 0.1 * level + 1e-06)
    keep = jnp.concatenate(
        [
            jnp.broadcast_to(
                jnp.where(
                    (bins >= band_lo[k]) & (bins < jnp.where(live[k] == 1, band_hi[k], 0)), 1.0, 0.0
                ),
                (SEG, BINS),
            )
            for k in range(count)
        ],
        axis=0,
    )
    factor = factor * keep
    out[:, :BINS] = (re * factor).astype(jnp.bfloat16)
    out[:, BINS:] = (im * factor).astype(jnp.bfloat16)


def whiten(traces, offsets, band_lo, band_hi, live):
    count = traces.shape[0]
    tables = (wave_rows(), eighth_table())
    return pl.pallas_call(
        whiten_kernel,
        out_shape=pltpu.VMEM((count * SEG, 2 * BINS), jnp.bfloat16),
        in_specs=[SMEM] * 4 + [VMEM] * 3,
        out_specs=VMEM,
        scratch_shapes=[pltpu.VMEM((4 * count * SEG, QUARTER), jnp.float32)],
        name="whiten",
    )(offsets, band_lo, band_hi, live, traces, *(jnp.asarray(table) for table in tables))


def cross_spectra(first_refs, left, right, cross, wide):
    at = 0
    for ref in first_refs:
        left[at : at + ref.shape[0], :] = ref[...].astype(jnp.float32)
        at += ref.shape[0]

    @pl.loop(0, left.shape[0] // SEG, unroll=4)
    def _(i):
        there = pl.ds(pl.multiple_of(i * wide, wide), wide)
        segments = pl.ds(pl.multiple_of(i * SEG, SEG), SEG)
        for t in range(BINS // LANES):
            re = pl.ds(t * LANES, LANES)
            im = pl.ds(BINS + t * LANES, LANES)
            cross_re = jnp.zeros((wide, LANES), jnp.float32)
            cross_im = jnp.zeros((wide, LANES), jnp.float32)
            rows_re, rows_im = left[segments, re], left[segments, im]
            for s in range(SEG):
                left_re, left_im = rows_re[s : s + 1, :], rows_im[s : s + 1, :]
                right_re = right[t, s * wide : (s + 1) * wide, :]
                right_im = right[t + BINS // LANES, s * wide : (s + 1) * wide, :]
                cross_re = cross_re + (left_re * right_re + left_im * right_im)
                cross_im = cross_im + (left_im * right_re - left_re * right_im)
            cross[there, re] = cross_re
            cross[there, im] = cross_im


def join_kernel(own, other, out):
    out[: own.shape[0], :] = own[...]
    out[own.shape[0] :, :] = other[...]


def join(own, other, cost=10**6):
    return pl.pallas_call(
        join_kernel,
        out_shape=pltpu.VMEM((own.shape[0] + other.shape[0], own.shape[1]), own.dtype),
        in_specs=[VMEM] * 2,
        out_specs=VMEM,
        cost_estimate=pl.CostEstimate(flops=cost, bytes_accessed=cost // 100, transcendentals=0),
        name="join",
    )(in_vmem(own), in_vmem(other))


def correlations(cross, table, out, row_masks):
    count = out.shape[3]
    high, low = split(cross[...])
    both = dot(jnp.concatenate([high, low], axis=0), table[...])
    corr = (both[: high.shape[0]] + both[high.shape[0] :]).astype(jnp.bfloat16)
    row_index = lax.axis_index("row")
    at = 0
    for i in range(out.shape[0]):
        for row_mask in row_masks:
            out[i, 0, row_index ^ row_mask] = corr[at : at + count, :]
            at += count


def prepare_kernel(count, second_parts, first_parts, row_masks, *refs):
    n_second = len(second_parts)
    second_refs = [ref.at[part, :] for ref, part in zip(refs[:n_second], second_parts, strict=True)]
    table, *first_refs, right, ready, left, cross = refs[n_second:]
    first_refs = [ref.at[part, :] for ref, part in zip(first_refs, first_parts, strict=True)]
    wide = count * len(row_masks)
    n = 0
    for ref in second_refs:
        for at in range(0, ref.shape[0], SEG):
            rows = ref[at : at + SEG, :].astype(jnp.float32)
            for t in range(2 * BINS // LANES):
                right[t, pl.ds(n, SEG, stride=wide), :] = rows[:, t * LANES : (t + 1) * LANES]
            n += 1
    cross_spectra(first_refs, left, right, cross, wide)
    correlations(cross, table, ready, row_masks)


def prepare(count, row_masks, second, lags, first):
    n_row = len(row_masks)
    parts = [tuple(part for _, part in blocks) for blocks in (second, first)]
    rows = sum(part.size for part in parts[1])
    return pl.pallas_call(
        functools.partial(prepare_kernel, count, *parts, row_masks),
        out_shape=(
            pltpu.VMEM((2 * BINS // LANES, count * n_row * SEG, LANES), jnp.float32),
            pltpu.VMEM((rows // SEG, 1, n_row, count, LAGS), jnp.bfloat16),
        ),
        in_specs=[VMEM] * (len(second) + 1 + len(first)),
        out_specs=(VMEM, VMEM),
        scratch_shapes=[
            pltpu.VMEM((rows, 2 * BINS), jnp.float32),
            pltpu.VMEM((rows // SEG * count * n_row, 2 * BINS), jnp.float32),
        ],
        name="prepare",
    )(*(in_vmem(block) for block, _ in second), in_vmem(lags), *(in_vmem(block) for block, _ in first))


def stage_kernel(row_masks, right, table, *refs):
    *first_refs, ready, left, cross = refs
    cross_spectra(first_refs, left, right, cross, right.shape[1] // SEG)
    correlations(cross, table, ready, row_masks)


def stage(count, row_masks, right, lags, first):
    n_row = len(row_masks)
    rows = sum(block.shape[0] for block in first)
    return pl.pallas_call(
        functools.partial(stage_kernel, row_masks),
        out_shape=pltpu.VMEM((rows // SEG, 1, n_row, count, LAGS), jnp.bfloat16),
        in_specs=[VMEM] * (2 + len(first)),
        out_specs=VMEM,
        scratch_shapes=[
            pltpu.VMEM((rows, 2 * BINS), jnp.float32),
            pltpu.VMEM((rows // SEG * count * n_row, 2 * BINS), jnp.float32),
        ],
        name="stage",
    )(*(in_vmem(block) for block in (right, lags, *first)))


def correlate_kernel(count, n_ready, masks, bits, row_masks, *refs):
    ready = refs[:n_ready]
    right, table, *first_refs, out, left, cross, last, sent = refs[n_ready:]
    col_index = lax.axis_index("col")
    cols = [at for mask in masks for at in spread(col_index ^ mask, bits)]
    blocks = [
        ref.at[pl.ds(at, count)] for ref in (*ready, last) for at in range(0, ref.shape[0], count)
    ]
    copies = [
        pltpu.make_async_copy(block, out.at[pl.ds(col * count, count)], sent.at[n])
        for n, (block, col) in enumerate(zip(blocks, cols, strict=True))
    ]
    early = len(blocks) - last.shape[0] // count
    for copy in copies[:early]:
        copy.start()
    cross_spectra(first_refs, left, right, cross, count * len(row_masks))
    correlations(cross, table, last, row_masks)
    for copy in copies[early:]:
        copy.start()
    for copy in copies:
        copy.wait()


def correlate(count, n_row, n_col, masks, bits, row_masks, ready, right, lags, first):
    channels, wide = count * n_col, count * n_row
    rows = sum(block.shape[0] for block in first)
    return pl.pallas_call(
        functools.partial(correlate_kernel, count, len(ready), masks, bits, row_masks),
        out_shape=jax.ShapeDtypeStruct((channels, 1, n_row, count, LAGS), jnp.bfloat16),
        in_specs=[VMEM] * (len(ready) + 2 + len(first)),
        out_specs=pl.BlockSpec(memory_space=pl.ANY),
        scratch_shapes=[
            pltpu.VMEM((rows, 2 * BINS), jnp.float32),
            pltpu.VMEM((rows // SEG * wide, 2 * BINS), jnp.float32),
            pltpu.VMEM((rows // SEG, 1, n_row, count, LAGS), jnp.bfloat16),
            pltpu.SemaphoreType.DMA((n_col,)),
        ],
        name="correlate",
    )(*(in_vmem(block) for block in (*ready, right, lags, *first)))


def swap(block, row_mask, col_mask):
    n_row, n_col = lax.axis_size("row"), lax.axis_size("col")
    pairs = [
        (row * n_col + col, (row ^ row_mask) * n_col + (col ^ col_mask))
        for row in range(n_row)
        for col in range(n_col)
    ]
    return lax.ppermute(block, ("row", "col"), pairs)


def spread(col, bits):
    cols = [col]
    for bit in bits:
        cols += [at ^ bit for at in cols]
    return cols


def body(traces, offsets, band_lo, band_hi, live):
    count = traces.shape[0]
    n_row, n_col = lax.axis_size("row"), lax.axis_size("col")
    white = whiten(traces, offsets, band_lo, band_hi, live)
    own, bits = white, []
    bit = n_col // 2
    while bit >= GROUP:
        own = join(own, swap(own, 0, bit))
        bits.append(bit)
        bit //= 2
    far = swap(own, 1, FAR)
    sibling = swap(own, 1, 0)
    across = swap(white, 2, 0)
    pair = join(far, sibling, 10**9)
    near = [swap(pair, 1, step) for step in STEPS]
    other, diagonal = swap(far, 1, 0), swap(across, 1, 0)
    rows, held = white.shape[0], own.shape[0]
    second = [(block, pl.ds(0, rows)) for block in (white, sibling, across, diagonal)]
    row_masks = [0, 1, 2, 3]
    if n_row > len(row_masks):
        stacked = jnp.concatenate([block[part.start : part.start + rows] for block, part in second])
        second = [(stacked, pl.ds(0, stacked.shape[0]))]
        bit = len(row_masks)
        while bit < n_row:
            second += [
                (swap(block, bit, 0), pl.ds(0, block.shape[0])) for block, _ in second
            ]
            row_masks += [mask ^ bit for mask in row_masks]
            bit *= 2
    lags = jnp.asarray(lag_table())
    first = [(own, pl.ds(0, held)), (other, pl.ds(0, held))]
    right, *ready = prepare(count, row_masks, second, lags, first)
    ready += [stage(count, row_masks, right, lags, near[-2::-1])]
    masks = [0, FAR, *(mask for step in (*STEPS[-2::-1], STEPS[-1]) for mask in (step ^ FAR, step))]
    return correlate(count, n_row, n_col, masks, bits, row_masks, ready, right, lags, near[-1:])


def solution(mesh):
    in_specs = (
        P(("row", "col"), None),
        P(("row", "col"), None),
        P(("row", "col")),
        P(("row", "col")),
        P(("row", "col")),
    )
    out_specs = P("row", "col", None, None, None)
    return jax.shard_map(body, mesh=mesh, in_specs=in_specs, out_specs=out_specs, check_vma=False)
```

```python
import functools
import math

import jax
import jax.numpy as jnp
import numpy as np
from jax import lax
from jax.experimental import pallas as pl
from jax.experimental.pallas import tpu as pltpu
from jax.sharding import PartitionSpec as P

SEG = 8
SAMPLES = 1024
BINS = 256
LAGS = 512
QUARTER = SAMPLES // 4
EIGHTH = SAMPLES // 8
LANES = 128
GROUP = 8
FAR = 6
STEPS = (3, 1, 2)
VMEM = pl.BlockSpec(memory_space=pltpu.VMEM)
SMEM = pl.BlockSpec(memory_space=pltpu.SMEM)


def split(values):
    high = values.astype(jnp.bfloat16)
    return high, (values - high.astype(jnp.float32)).astype(jnp.bfloat16)


def split_table(table):
    high = table.astype(jnp.bfloat16)
    return np.stack([high, (table - high.astype(np.float64)).astype(jnp.bfloat16)])


def eighth_table():
    times = np.arange(EIGHTH)
    freqs = np.arange(BINS) + 1
    phase = (times[:, None] * freqs[None, :] % SAMPLES) * (2.0 * math.pi / SAMPLES)
    return split_table(np.concatenate([np.cos(phase), -np.sin(phase)], axis=1))


def wave_rows():
    times = np.arange(SAMPLES) * (2.0 * math.pi / SAMPLES)
    freqs = np.arange(BINS) + 1
    eighth = (freqs % 8) * (math.pi / 4.0)
    cos_turn = np.array([1.0, 0.0, -1.0, 0.0])[freqs % 4]
    sin_turn = np.array([0.0, 1.0, 0.0, -1.0])[freqs % 4]
    taper = (0.5 - 0.5 * np.cos(times)).reshape(4, QUARTER)
    return np.stack([*taper, cos_turn, sin_turn, np.cos(eighth), np.sin(eighth)]).astype(np.float32)


def lag_table():
    freqs = np.arange(BINS) + 1
    shifts = np.arange(LAGS) - LAGS // 2
    phase = (freqs[:, None] * shifts[None, :] % SAMPLES) * (2.0 * math.pi / SAMPLES)
    table = np.concatenate([np.cos(phase), -np.sin(phase)], axis=0)
    return (table / math.sqrt(SEG * BINS)).astype(jnp.bfloat16)


def in_vmem(array):
    return pltpu.with_memory_space_constraint(array, pltpu.VMEM)


def dot(left, right):
    return jnp.dot(left, right, preferred_element_type=jnp.float32)


def whiten_kernel(offsets, band_lo, band_hi, live, traces, waves, table, out, quarters):
    count = traces.shape[0]
    rows = count * SEG
    for k in range(count):
        for s in range(SEG):
            start = pl.multiple_of(offsets[k, s], QUARTER)
            segment = traces[pl.ds(k, 1), pl.ds(start, SAMPLES)]
            for q in range(4):
                quarters[pl.ds(q * rows + k * SEG + s, 1), :] = segment[
                    :, q * QUARTER : (q + 1) * QUARTER
                ]
    parts = jnp.concatenate(
        [quarters[q * rows : (q + 1) * rows, :] * waves[q : q + 1, :] for q in range(4)], axis=0
    )
    high, low = split(jnp.concatenate([parts[:, :EIGHTH], parts[:, EIGHTH:]], axis=0))
    spectra = dot(
        jnp.concatenate([high, low, high], axis=1),
        jnp.concatenate([table[0], table[0], table[1]], axis=0),
    )
    cos_turn, sin_turn = waves[4:5, :], waves[5:6, :]
    sign = cos_turn * cos_turn - sin_turn * sin_turn

    def turned(n):
        quarter = [spectra[(n + q) * rows : (n + q + 1) * rows] for q in range(4)]
        re, im = [x[:, :BINS] for x in quarter], [x[:, BINS:] for x in quarter]
        return (
            (re[0] + re[2] * sign) + ((re[1] + re[3]) * cos_turn + (im[1] - im[3]) * sin_turn),
            (im[0] + im[2] * sign) + ((im[1] + im[3]) * cos_turn + (re[3] - re[1]) * sin_turn),
        )

    early_re, early_im = turned(0)
    late_re, late_im = turned(4)
    cos_eighth, sin_eighth = waves[6:7, :], waves[7:8, :]
    re = early_re + (late_re * cos_eighth + late_im * sin_eighth)
    im = early_im + (late_im * cos_eighth - late_re * sin_eighth)
    amp = jnp.sqrt(re * re + im * im)
    bins = lax.broadcasted_iota(jnp.int32, (1, BINS), 1)
    total = amp
    for step in (1, 2):
        total = total + jnp.where(bins >= step, pltpu.roll(amp, step, 1), 0.0)
        total = total + jnp.where(bins < BINS - step, pltpu.roll(amp, BINS - step, 1), 0.0)
    level = jnp.sum(amp, axis=1, keepdims=True) * (1.0 / BINS)
    factor = 1.0 / (total / 5.0 + 0.1 * level + 1e-06)
    keep = jnp.concatenate(
        [
            jnp.broadcast_to(
                jnp.where(
                    (bins >= band_lo[k]) & (bins < jnp.where(live[k] == 1, band_hi[k], 0)), 1.0, 0.0
                ),
                (SEG, BINS),
            )
            for k in range(count)
        ],
        axis=0,
    )
    factor = factor * keep
    out[:, :BINS] = (re * factor).astype(jnp.bfloat16)
    out[:, BINS:] = (im * factor).astype(jnp.bfloat16)


def whiten(traces, offsets, band_lo, band_hi, live):
    count = traces.shape[0]
    tables = (wave_rows(), eighth_table())
    return pl.pallas_call(
        whiten_kernel,
        out_shape=pltpu.VMEM((count * SEG, 2 * BINS), jnp.bfloat16),
        in_specs=[SMEM] * 4 + [VMEM] * 3,
        out_specs=VMEM,
        scratch_shapes=[pltpu.VMEM((4 * count * SEG, QUARTER), jnp.float32)],
        name="whiten",
    )(offsets, band_lo, band_hi, live, traces, *(jnp.asarray(table) for table in tables))


def cross_spectra(first_refs, left, right, cross, wide):
    at = 0
    for ref in first_refs:
        left[at : at + ref.shape[0], :] = ref[...].astype(jnp.float32)
        at += ref.shape[0]

    @pl.loop(0, left.shape[0] // SEG, unroll=4)
    def _(i):
        there = pl.ds(pl.multiple_of(i * wide, wide), wide)
        segments = pl.ds(pl.multiple_of(i * SEG, SEG), SEG)
        for t in range(BINS // LANES):
            re = pl.ds(t * LANES, LANES)
            im = pl.ds(BINS + t * LANES, LANES)
            cross_re = jnp.zeros((wide, LANES), jnp.float32)
            cross_im = jnp.zeros((wide, LANES), jnp.float32)
            rows_re, rows_im = left[segments, re], left[segments, im]
            for s in range(SEG):
                left_re, left_im = rows_re[s : s + 1, :], rows_im[s : s + 1, :]
                right_re = right[t, s * wide : (s + 1) * wide, :]
                right_im = right[t + BINS // LANES, s * wide : (s + 1) * wide, :]
                cross_re = cross_re + (left_re * right_re + left_im * right_im)
                cross_im = cross_im + (left_im * right_re - left_re * right_im)
            cross[there, re] = cross_re
            cross[there, im] = cross_im


def join_kernel(own, other, out):
    out[: own.shape[0], :] = own[...]
    out[own.shape[0] :, :] = other[...]


def join(own, other, cost=10**6):
    return pl.pallas_call(
        join_kernel,
        out_shape=pltpu.VMEM((own.shape[0] + other.shape[0], own.shape[1]), own.dtype),
        in_specs=[VMEM] * 2,
        out_specs=VMEM,
        cost_estimate=pl.CostEstimate(flops=cost, bytes_accessed=cost // 100, transcendentals=0),
        name="join",
    )(in_vmem(own), in_vmem(other))


def correlations(cross, table, out, row_masks):
    count = out.shape[3]
    high, low = split(cross[...])
    both = dot(jnp.concatenate([high, low], axis=0), table[...])
    corr = (both[: high.shape[0]] + both[high.shape[0] :]).astype(jnp.bfloat16)
    row_index = lax.axis_index("row")
    at = 0
    for i in range(out.shape[0]):
        for row_mask in row_masks:
            out[i, 0, row_index ^ row_mask] = corr[at : at + count, :]
            at += count


def prepare_kernel(count, second_parts, first_parts, row_masks, *refs):
    n_second = len(second_parts)
    second_refs = [ref.at[part, :] for ref, part in zip(refs[:n_second], second_parts, strict=True)]
    table, *first_refs, right, ready, left, cross = refs[n_second:]
    first_refs = [ref.at[part, :] for ref, part in zip(first_refs, first_parts, strict=True)]
    wide = count * len(row_masks)
    n = 0
    for ref in second_refs:
        for at in range(0, ref.shape[0], SEG):
            rows = ref[at : at + SEG, :].astype(jnp.float32)
            for t in range(2 * BINS // LANES):
                right[t, pl.ds(n, SEG, stride=wide), :] = rows[:, t * LANES : (t + 1) * LANES]
            n += 1
    cross_spectra(first_refs, left, right, cross, wide)
    correlations(cross, table, ready, row_masks)


def prepare(count, row_masks, second, lags, first):
    n_row = len(row_masks)
    parts = [tuple(part for _, part in blocks) for blocks in (second, first)]
    rows = sum(part.size for part in parts[1])
    return pl.pallas_call(
        functools.partial(prepare_kernel, count, *parts, row_masks),
        out_shape=(
            pltpu.VMEM((2 * BINS // LANES, count * n_row * SEG, LANES), jnp.float32),
            pltpu.VMEM((rows // SEG, 1, n_row, count, LAGS), jnp.bfloat16),
        ),
        in_specs=[VMEM] * (len(second) + 1 + len(first)),
        out_specs=(VMEM, VMEM),
        scratch_shapes=[
            pltpu.VMEM((rows, 2 * BINS), jnp.float32),
            pltpu.VMEM((rows // SEG * count * n_row, 2 * BINS), jnp.float32),
        ],
        name="prepare",
    )(*(in_vmem(block) for block, _ in second), in_vmem(lags), *(in_vmem(block) for block, _ in first))


def stage_kernel(row_masks, right, table, *refs):
    *first_refs, ready, left, cross = refs
    cross_spectra(first_refs, left, right, cross, right.shape[1] // SEG)
    correlations(cross, table, ready, row_masks)


def stage(count, row_masks, right, lags, first):
    n_row = len(row_masks)
    rows = sum(block.shape[0] for block in first)
    return pl.pallas_call(
        functools.partial(stage_kernel, row_masks),
        out_shape=pltpu.VMEM((rows // SEG, 1, n_row, count, LAGS), jnp.bfloat16),
        in_specs=[VMEM] * (2 + len(first)),
        out_specs=VMEM,
        scratch_shapes=[
            pltpu.VMEM((rows, 2 * BINS), jnp.float32),
            pltpu.VMEM((rows // SEG * count * n_row, 2 * BINS), jnp.float32),
        ],
        name="stage",
    )(*(in_vmem(block) for block in (right, lags, *first)))


def correlate_kernel(count, n_ready, masks, bits, row_masks, *refs):
    ready = refs[:n_ready]
    right, table, *first_refs, out, left, cross, last, sent = refs[n_ready:]
    col_index = lax.axis_index("col")
    cols = [at for mask in masks for at in spread(col_index ^ mask, bits)]
    blocks = [
        ref.at[pl.ds(at, count)] for ref in (*ready, last) for at in range(0, ref.shape[0], count)
    ]
    copies = [
        pltpu.make_async_copy(block, out.at[pl.ds(col * count, count)], sent.at[n])
        for n, (block, col) in enumerate(zip(blocks, cols, strict=True))
    ]
    early = len(blocks) - last.shape[0] // count
    for copy in copies[:early]:
        copy.start()
    cross_spectra(first_refs, left, right, cross, count * len(row_masks))
    correlations(cross, table, last, row_masks)
    for copy in copies[early:]:
        copy.start()
    for copy in copies:
        copy.wait()


def correlate(count, n_row, n_col, masks, bits, row_masks, ready, right, lags, first):
    channels, wide = count * n_col, count * n_row
    rows = sum(block.shape[0] for block in first)
    return pl.pallas_call(
        functools.partial(correlate_kernel, count, len(ready), masks, bits, row_masks),
        out_shape=jax.ShapeDtypeStruct((channels, 1, n_row, count, LAGS), jnp.bfloat16),
        in_specs=[VMEM] * (len(ready) + 2 + len(first)),
        out_specs=pl.BlockSpec(memory_space=pl.ANY),
        scratch_shapes=[
            pltpu.VMEM((rows, 2 * BINS), jnp.float32),
            pltpu.VMEM((rows // SEG * wide, 2 * BINS), jnp.float32),
            pltpu.VMEM((rows // SEG, 1, n_row, count, LAGS), jnp.bfloat16),
            pltpu.SemaphoreType.DMA((n_col,)),
        ],
        name="correlate",
    )(*(in_vmem(block) for block in (*ready, right, lags, *first)))


def swap(block, row_mask, col_mask):
    n_row, n_col = lax.axis_size("row"), lax.axis_size("col")
    pairs = [
        (row * n_col + col, (row ^ row_mask) * n_col + (col ^ col_mask))
        for row in range(n_row)
        for col in range(n_col)
    ]
    return lax.ppermute(block, ("row", "col"), pairs)


def spread(col, bits):
    cols = [col]
    for bit in bits:
        cols += [at ^ bit for at in cols]
    return cols


def body(traces, offsets, band_lo, band_hi, live):
    count = traces.shape[0]
    n_row, n_col = lax.axis_size("row"), lax.axis_size("col")
    white = whiten(traces, offsets, band_lo, band_hi, live)
    own, bits = white, []
    bit = n_col // 2
    while bit >= GROUP:
        own = join(own, swap(own, 0, bit))
        bits.append(bit)
        bit //= 2
    far = swap(own, 1, FAR)
    sibling = swap(own, 1, 0)
    across = swap(white, 3, 0)
    pair = join(far, sibling, 10**9)
    near = [swap(pair, 1, step) for step in STEPS]
    other, diagonal = swap(far, 1, 0), swap(across, 1, 0)
    rows, held = white.shape[0], own.shape[0]
    second = [(block, pl.ds(0, rows)) for block in (white, sibling, across, diagonal)]
    row_masks = [0, 1, 3, 2]
    if n_row > len(row_masks):
        stacked = jnp.concatenate([block[part.start : part.start + rows] for block, part in second])
        second = [(stacked, pl.ds(0, stacked.shape[0]))]
        bit = len(row_masks)
        while bit < n_row:
            second += [
                (swap(block, bit, 0), pl.ds(0, block.shape[0])) for block, _ in second
            ]
            row_masks += [mask ^ bit for mask in row_masks]
            bit *= 2
    lags = jnp.asarray(lag_table())
    right, *ready = prepare(count, row_masks, second, lags, [(own, pl.ds(0, held))])
    ready += [stage(count, row_masks, right, lags, [other, near[0]])]
    masks = [0, FAR]
    for step in (STEPS[0], *STEPS[:0:-1]):
        masks += [step ^ FAR, step]
    last = near[:0:-1]
    return correlate(count, n_row, n_col, masks, bits, row_masks, ready, right, lags, last)


def solution(mesh):
    in_specs = (
        P(("row", "col"), None),
        P(("row", "col"), None),
        P(("row", "col")),
        P(("row", "col")),
        P(("row", "col")),
    )
    out_specs = P("row", "col", None, None, None)
    return jax.shard_map(body, mesh=mesh, in_specs=in_specs, out_specs=out_specs, check_vma=False)
```

```python
import functools
import math

import jax
import jax.numpy as jnp
import numpy as np
from jax import lax
from jax.experimental import pallas as pl
from jax.experimental.pallas import tpu as pltpu
from jax.sharding import PartitionSpec as P

SEG = 8
SAMPLES = 1024
BINS = 256
LAGS = 512
QUARTER = SAMPLES // 4
EIGHTH = SAMPLES // 8
LANES = 128
GROUP = 8
FAR = 4
STEPS = (3, 2, 1)
VMEM = pl.BlockSpec(memory_space=pltpu.VMEM)
SMEM = pl.BlockSpec(memory_space=pltpu.SMEM)


def split(values):
    high = values.astype(jnp.bfloat16)
    return high, (values - high.astype(jnp.float32)).astype(jnp.bfloat16)


def split_table(table):
    high = table.astype(jnp.bfloat16)
    return np.stack([high, (table - high.astype(np.float64)).astype(jnp.bfloat16)])


def eighth_table():
    times = np.arange(EIGHTH)
    freqs = np.arange(BINS) + 1
    phase = (times[:, None] * freqs[None, :] % SAMPLES) * (2.0 * math.pi / SAMPLES)
    return split_table(np.concatenate([np.cos(phase), -np.sin(phase)], axis=1))


def wave_rows():
    times = np.arange(SAMPLES) * (2.0 * math.pi / SAMPLES)
    freqs = np.arange(BINS) + 1
    eighth = (freqs % 8) * (math.pi / 4.0)
    cos_turn = np.array([1.0, 0.0, -1.0, 0.0])[freqs % 4]
    sin_turn = np.array([0.0, 1.0, 0.0, -1.0])[freqs % 4]
    taper = (0.5 - 0.5 * np.cos(times)).reshape(4, QUARTER)
    return np.stack([*taper, cos_turn, sin_turn, np.cos(eighth), np.sin(eighth)]).astype(np.float32)


def lag_table():
    freqs = np.arange(BINS) + 1
    shifts = np.arange(LAGS) - LAGS // 2
    phase = (freqs[:, None] * shifts[None, :] % SAMPLES) * (2.0 * math.pi / SAMPLES)
    table = np.concatenate([np.cos(phase), -np.sin(phase)], axis=0)
    return (table / math.sqrt(SEG * BINS)).astype(jnp.bfloat16)


def in_vmem(array):
    return pltpu.with_memory_space_constraint(array, pltpu.VMEM)


def dot(left, right):
    return jnp.dot(left, right, preferred_element_type=jnp.float32)


def whiten_kernel(offsets, band_lo, band_hi, live, traces, waves, table, out, quarters):
    count = traces.shape[0]
    rows = count * SEG
    for k in range(count):
        for s in range(SEG):
            start = pl.multiple_of(offsets[k, s], QUARTER)
            segment = traces[pl.ds(k, 1), pl.ds(start, SAMPLES)]
            for q in range(4):
                quarters[pl.ds(q * rows + k * SEG + s, 1), :] = segment[
                    :, q * QUARTER : (q + 1) * QUARTER
                ]
    parts = jnp.concatenate(
        [quarters[q * rows : (q + 1) * rows, :] * waves[q : q + 1, :] for q in range(4)], axis=0
    )
    high, low = split(jnp.concatenate([parts[:, :EIGHTH], parts[:, EIGHTH:]], axis=0))
    spectra = dot(
        jnp.concatenate([high, low, high], axis=1),
        jnp.concatenate([table[0], table[0], table[1]], axis=0),
    )
    cos_turn, sin_turn = waves[4:5, :], waves[5:6, :]
    sign = cos_turn * cos_turn - sin_turn * sin_turn

    def turned(n):
        quarter = [spectra[(n + q) * rows : (n + q + 1) * rows] for q in range(4)]
        re, im = [x[:, :BINS] for x in quarter], [x[:, BINS:] for x in quarter]
        return (
            (re[0] + re[2] * sign) + ((re[1] + re[3]) * cos_turn + (im[1] - im[3]) * sin_turn),
            (im[0] + im[2] * sign) + ((im[1] + im[3]) * cos_turn + (re[3] - re[1]) * sin_turn),
        )

    early_re, early_im = turned(0)
    late_re, late_im = turned(4)
    cos_eighth, sin_eighth = waves[6:7, :], waves[7:8, :]
    re = early_re + (late_re * cos_eighth + late_im * sin_eighth)
    im = early_im + (late_im * cos_eighth - late_re * sin_eighth)
    amp = jnp.sqrt(re * re + im * im)
    bins = lax.broadcasted_iota(jnp.int32, (1, BINS), 1)
    total = amp
    for step in (1, 2):
        total = total + jnp.where(bins >= step, pltpu.roll(amp, step, 1), 0.0)
        total = total + jnp.where(bins < BINS - step, pltpu.roll(amp, BINS - step, 1), 0.0)
    level = jnp.sum(amp, axis=1, keepdims=True) * (1.0 / BINS)
    factor = 1.0 / (total / 5.0 + 0.1 * level + 1e-06)
    keep = jnp.concatenate(
        [
            jnp.broadcast_to(
                jnp.where(
                    (bins >= band_lo[k]) & (bins < jnp.where(live[k] == 1, band_hi[k], 0)), 1.0, 0.0
                ),
                (SEG, BINS),
            )
            for k in range(count)
        ],
        axis=0,
    )
    factor = factor * keep
    out[:, :BINS] = (re * factor).astype(jnp.bfloat16)
    out[:, BINS:] = (im * factor).astype(jnp.bfloat16)


def whiten(traces, offsets, band_lo, band_hi, live):
    count = traces.shape[0]
    tables = (wave_rows(), eighth_table())
    return pl.pallas_call(
        whiten_kernel,
        out_shape=pltpu.VMEM((count * SEG, 2 * BINS), jnp.bfloat16),
        in_specs=[SMEM] * 4 + [VMEM] * 3,
        out_specs=VMEM,
        scratch_shapes=[pltpu.VMEM((4 * count * SEG, QUARTER), jnp.float32)],
        name="whiten",
    )(offsets, band_lo, band_hi, live, traces, *(jnp.asarray(table) for table in tables))


def cross_spectra(first_refs, left, right, cross, wide):
    at = 0
    for ref in first_refs:
        left[at : at + ref.shape[0], :] = ref[...].astype(jnp.float32)
        at += ref.shape[0]

    @pl.loop(0, left.shape[0] // SEG, unroll=4)
    def _(i):
        there = pl.ds(pl.multiple_of(i * wide, wide), wide)
        segments = pl.ds(pl.multiple_of(i * SEG, SEG), SEG)
        for t in range(BINS // LANES):
            re = pl.ds(t * LANES, LANES)
            im = pl.ds(BINS + t * LANES, LANES)
            cross_re = jnp.zeros((wide, LANES), jnp.float32)
            cross_im = jnp.zeros((wide, LANES), jnp.float32)
            rows_re, rows_im = left[segments, re], left[segments, im]
            for s in range(SEG):
                left_re, left_im = rows_re[s : s + 1, :], rows_im[s : s + 1, :]
                right_re = right[t, s * wide : (s + 1) * wide, :]
                right_im = right[t + BINS // LANES, s * wide : (s + 1) * wide, :]
                cross_re = cross_re + (left_re * right_re + left_im * right_im)
                cross_im = cross_im + (left_im * right_re - left_re * right_im)
            cross[there, re] = cross_re
            cross[there, im] = cross_im


def join_kernel(own, other, out):
    out[: own.shape[0], :] = own[...]
    out[own.shape[0] :, :] = other[...]


def join(own, other, cost=10**6):
    return pl.pallas_call(
        join_kernel,
        out_shape=pltpu.VMEM((own.shape[0] + other.shape[0], own.shape[1]), own.dtype),
        in_specs=[VMEM] * 2,
        out_specs=VMEM,
        cost_estimate=pl.CostEstimate(flops=cost, bytes_accessed=cost // 100, transcendentals=0),
        name="join",
    )(in_vmem(own), in_vmem(other))


def correlations(cross, table, out, row_masks):
    count = out.shape[3]
    high, low = split(cross[...])
    both = dot(jnp.concatenate([high, low], axis=0), table[...])
    corr = (both[: high.shape[0]] + both[high.shape[0] :]).astype(jnp.bfloat16)
    row_index = lax.axis_index("row")
    at = 0
    for i in range(out.shape[0]):
        for row_mask in row_masks:
            out[i, 0, row_index ^ row_mask] = corr[at : at + count, :]
            at += count


def prepare_kernel(count, second_parts, first_parts, row_masks, *refs):
    n_second = len(second_parts)
    second_refs = [ref.at[part, :] for ref, part in zip(refs[:n_second], second_parts, strict=True)]
    table, *first_refs, right, ready, left, cross = refs[n_second:]
    first_refs = [ref.at[part, :] for ref, part in zip(first_refs, first_parts, strict=True)]
    wide = count * len(row_masks)
    n = 0
    for ref in second_refs:
        for at in range(0, ref.shape[0], SEG):
            rows = ref[at : at + SEG, :].astype(jnp.float32)
            for t in range(2 * BINS // LANES):
                right[t, pl.ds(n, SEG, stride=wide), :] = rows[:, t * LANES : (t + 1) * LANES]
            n += 1
    cross_spectra(first_refs, left, right, cross, wide)
    correlations(cross, table, ready, row_masks)


def prepare(count, row_masks, second, lags, first):
    n_row = len(row_masks)
    parts = [tuple(part for _, part in blocks) for blocks in (second, first)]
    rows = sum(part.size for part in parts[1])
    return pl.pallas_call(
        functools.partial(prepare_kernel, count, *parts, row_masks),
        out_shape=(
            pltpu.VMEM((2 * BINS // LANES, count * n_row * SEG, LANES), jnp.float32),
            pltpu.VMEM((rows // SEG, 1, n_row, count, LAGS), jnp.bfloat16),
        ),
        in_specs=[VMEM] * (len(second) + 1 + len(first)),
        out_specs=(VMEM, VMEM),
        scratch_shapes=[
            pltpu.VMEM((rows, 2 * BINS), jnp.float32),
            pltpu.VMEM((rows // SEG * count * n_row, 2 * BINS), jnp.float32),
        ],
        name="prepare",
    )(*(in_vmem(block) for block, _ in second), in_vmem(lags), *(in_vmem(block) for block, _ in first))


def stage_kernel(row_masks, right, table, *refs):
    *first_refs, ready, left, cross = refs
    cross_spectra(first_refs, left, right, cross, right.shape[1] // SEG)
    correlations(cross, table, ready, row_masks)


def stage(count, row_masks, right, lags, first):
    n_row = len(row_masks)
    rows = sum(block.shape[0] for block in first)
    return pl.pallas_call(
        functools.partial(stage_kernel, row_masks),
        out_shape=pltpu.VMEM((rows // SEG, 1, n_row, count, LAGS), jnp.bfloat16),
        in_specs=[VMEM] * (2 + len(first)),
        out_specs=VMEM,
        scratch_shapes=[
            pltpu.VMEM((rows, 2 * BINS), jnp.float32),
            pltpu.VMEM((rows // SEG * count * n_row, 2 * BINS), jnp.float32),
        ],
        name="stage",
    )(*(in_vmem(block) for block in (right, lags, *first)))


def correlate_kernel(count, n_ready, masks, bits, row_masks, *refs):
    ready = refs[:n_ready]
    right, table, *first_refs, out, left, cross, last, sent = refs[n_ready:]
    col_index = lax.axis_index("col")
    cols = [at for mask in masks for at in spread(col_index ^ mask, bits)]
    blocks = [
        ref.at[pl.ds(at, count)] for ref in (*ready, last) for at in range(0, ref.shape[0], count)
    ]
    copies = [
        pltpu.make_async_copy(block, out.at[pl.ds(col * count, count)], sent.at[n])
        for n, (block, col) in enumerate(zip(blocks, cols, strict=True))
    ]
    early = len(blocks) - last.shape[0] // count
    for copy in copies[:early]:
        copy.start()
    cross_spectra(first_refs, left, right, cross, count * len(row_masks))
    correlations(cross, table, last, row_masks)
    for copy in copies[early:]:
        copy.start()
    for copy in copies:
        copy.wait()


def correlate(count, n_row, n_col, masks, bits, row_masks, ready, right, lags, first):
    channels, wide = count * n_col, count * n_row
    rows = sum(block.shape[0] for block in first)
    return pl.pallas_call(
        functools.partial(correlate_kernel, count, len(ready), masks, bits, row_masks),
        out_shape=jax.ShapeDtypeStruct((channels, 1, n_row, count, LAGS), jnp.bfloat16),
        in_specs=[VMEM] * (len(ready) + 2 + len(first)),
        out_specs=pl.BlockSpec(memory_space=pl.ANY),
        scratch_shapes=[
            pltpu.VMEM((rows, 2 * BINS), jnp.float32),
            pltpu.VMEM((rows // SEG * wide, 2 * BINS), jnp.float32),
            pltpu.VMEM((rows // SEG, 1, n_row, count, LAGS), jnp.bfloat16),
            pltpu.SemaphoreType.DMA((n_col,)),
        ],
        name="correlate",
    )(*(in_vmem(block) for block in (*ready, right, lags, *first)))


def swap(block, row_mask, col_mask):
    n_row, n_col = lax.axis_size("row"), lax.axis_size("col")
    pairs = [
        (row * n_col + col, (row ^ row_mask) * n_col + (col ^ col_mask))
        for row in range(n_row)
        for col in range(n_col)
    ]
    return lax.ppermute(block, ("row", "col"), pairs)


def spread(col, bits):
    cols = [col]
    for bit in bits:
        cols += [at ^ bit for at in cols]
    return cols


def body(traces, offsets, band_lo, band_hi, live):
    count = traces.shape[0]
    n_row, n_col = lax.axis_size("row"), lax.axis_size("col")
    white = whiten(traces, offsets, band_lo, band_hi, live)
    own, bits = white, []
    bit = n_col // 2
    while bit >= GROUP:
        own = join(own, swap(own, 0, bit))
        bits.append(bit)
        bit //= 2
    far = swap(own, 1, FAR)
    sibling = swap(own, 1, 0)
    across = swap(white, 3, 0)
    pair = join(far, sibling, 10**9)
    near = [swap(pair, 1, step) for step in STEPS]
    other, diagonal = swap(far, 1, 0), swap(across, 1, 0)
    rows, held = white.shape[0], own.shape[0]
    second = [(block, pl.ds(0, rows)) for block in (white, sibling, across, diagonal)]
    row_masks = [0, 1, 3, 2]
    if n_row > len(row_masks):
        stacked = jnp.concatenate([block[part.start : part.start + rows] for block, part in second])
        second = [(stacked, pl.ds(0, stacked.shape[0]))]
        bit = len(row_masks)
        while bit < n_row:
            second += [
                (swap(block, bit, 0), pl.ds(0, block.shape[0])) for block, _ in second
            ]
            row_masks += [mask ^ bit for mask in row_masks]
            bit *= 2
    lags = jnp.asarray(lag_table())
    right, *ready = prepare(count, row_masks, second, lags, [(own, pl.ds(0, held))])
    ready += [stage(count, row_masks, right, lags, [other, near[0]])]
    masks = [0, FAR]
    for step in (STEPS[0], *STEPS[:0:-1]):
        masks += [step ^ FAR, step]
    last = near[:0:-1]
    return correlate(count, n_row, n_col, masks, bits, row_masks, ready, right, lags, last)


def solution(mesh):
    in_specs = (
        P(("row", "col"), None),
        P(("row", "col"), None),
        P(("row", "col")),
        P(("row", "col")),
        P(("row", "col")),
    )
    out_specs = P("row", "col", None, None, None)
    return jax.shard_map(body, mesh=mesh, in_specs=in_specs, out_specs=out_specs, check_vma=False)
```

```python
import functools
import math

import jax
import jax.numpy as jnp
import numpy as np
from jax import lax
from jax.experimental import pallas as pl
from jax.experimental.pallas import tpu as pltpu
from jax.sharding import PartitionSpec as P

SEG = 8
SAMPLES = 1024
BINS = 256
LAGS = 512
QUARTER = SAMPLES // 4
EIGHTH = SAMPLES // 8
LANES = 128
GROUP = 8
FAR = 4
STEPS = (3, 2, 1)
VMEM = pl.BlockSpec(memory_space=pltpu.VMEM)
SMEM = pl.BlockSpec(memory_space=pltpu.SMEM)


def split(values):
    high = values.astype(jnp.bfloat16)
    return high, (values - high.astype(jnp.float32)).astype(jnp.bfloat16)


def split_table(table):
    high = table.astype(jnp.bfloat16)
    return np.stack([high, (table - high.astype(np.float64)).astype(jnp.bfloat16)])


def eighth_table():
    times = np.arange(EIGHTH)
    freqs = np.arange(BINS) + 1
    phase = (times[:, None] * freqs[None, :] % SAMPLES) * (2.0 * math.pi / SAMPLES)
    return split_table(np.concatenate([np.cos(phase), -np.sin(phase)], axis=1))


def wave_rows():
    times = np.arange(SAMPLES) * (2.0 * math.pi / SAMPLES)
    freqs = np.arange(BINS) + 1
    eighth = (freqs % 8) * (math.pi / 4.0)
    cos_turn = np.array([1.0, 0.0, -1.0, 0.0])[freqs % 4]
    sin_turn = np.array([0.0, 1.0, 0.0, -1.0])[freqs % 4]
    taper = (0.5 - 0.5 * np.cos(times)).reshape(4, QUARTER)
    return np.stack([*taper, cos_turn, sin_turn, np.cos(eighth), np.sin(eighth)]).astype(np.float32)


def lag_table():
    freqs = np.arange(BINS) + 1
    shifts = np.arange(LAGS) - LAGS // 2
    phase = (freqs[:, None] * shifts[None, :] % SAMPLES) * (2.0 * math.pi / SAMPLES)
    table = np.concatenate([np.cos(phase), -np.sin(phase)], axis=0)
    return (table / math.sqrt(SEG * BINS)).astype(jnp.bfloat16)


def in_vmem(array):
    return pltpu.with_memory_space_constraint(array, pltpu.VMEM)


def dot(left, right):
    return jnp.dot(left, right, preferred_element_type=jnp.float32)


def whiten_kernel(offsets, band_lo, band_hi, live, traces, waves, table, out, quarters):
    count = traces.shape[0]
    rows = count * SEG
    for k in range(count):
        for s in range(SEG):
            start = pl.multiple_of(offsets[k, s], QUARTER)
            segment = traces[pl.ds(k, 1), pl.ds(start, SAMPLES)]
            for q in range(4):
                quarters[pl.ds(q * rows + k * SEG + s, 1), :] = segment[
                    :, q * QUARTER : (q + 1) * QUARTER
                ]
    parts = jnp.concatenate(
        [quarters[q * rows : (q + 1) * rows, :] * waves[q : q + 1, :] for q in range(4)], axis=0
    )
    high, low = split(jnp.concatenate([parts[:, :EIGHTH], parts[:, EIGHTH:]], axis=0))
    spectra = dot(
        jnp.concatenate([high, low, high], axis=1),
        jnp.concatenate([table[0], table[0], table[1]], axis=0),
    )
    cos_turn, sin_turn = waves[4:5, :], waves[5:6, :]
    sign = cos_turn * cos_turn - sin_turn * sin_turn

    def turned(n):
        quarter = [spectra[(n + q) * rows : (n + q + 1) * rows] for q in range(4)]
        re, im = [x[:, :BINS] for x in quarter], [x[:, BINS:] for x in quarter]
        return (
            (re[0] + re[2] * sign) + ((re[1] + re[3]) * cos_turn + (im[1] - im[3]) * sin_turn),
            (im[0] + im[2] * sign) + ((im[1] + im[3]) * cos_turn + (re[3] - re[1]) * sin_turn),
        )

    early_re, early_im = turned(0)
    late_re, late_im = turned(4)
    cos_eighth, sin_eighth = waves[6:7, :], waves[7:8, :]
    re = early_re + (late_re * cos_eighth + late_im * sin_eighth)
    im = early_im + (late_im * cos_eighth - late_re * sin_eighth)
    amp = jnp.sqrt(re * re + im * im)
    bins = lax.broadcasted_iota(jnp.int32, (1, BINS), 1)
    total = amp
    for step in (1, 2):
        total = total + jnp.where(bins >= step, pltpu.roll(amp, step, 1), 0.0)
        total = total + jnp.where(bins < BINS - step, pltpu.roll(amp, BINS - step, 1), 0.0)
    level = jnp.sum(amp, axis=1, keepdims=True) * (1.0 / BINS)
    factor = 1.0 / (total / 5.0 + 0.1 * level + 1e-06)
    keep = jnp.concatenate(
        [
            jnp.broadcast_to(
                jnp.where(
                    (bins >= band_lo[k]) & (bins < jnp.where(live[k] == 1, band_hi[k], 0)), 1.0, 0.0
                ),
                (SEG, BINS),
            )
            for k in range(count)
        ],
        axis=0,
    )
    factor = factor * keep
    out[:, :BINS] = (re * factor).astype(jnp.bfloat16)
    out[:, BINS:] = (im * factor).astype(jnp.bfloat16)


def whiten(traces, offsets, band_lo, band_hi, live):
    count = traces.shape[0]
    tables = (wave_rows(), eighth_table())
    return pl.pallas_call(
        whiten_kernel,
        out_shape=pltpu.VMEM((count * SEG, 2 * BINS), jnp.bfloat16),
        in_specs=[SMEM] * 4 + [VMEM] * 3,
        out_specs=VMEM,
        scratch_shapes=[pltpu.VMEM((4 * count * SEG, QUARTER), jnp.float32)],
        name="whiten",
    )(offsets, band_lo, band_hi, live, traces, *(jnp.asarray(table) for table in tables))


def cross_spectra(first_refs, left, right, cross, wide):
    at = 0
    for ref in first_refs:
        left[at : at + ref.shape[0], :] = ref[...].astype(jnp.float32)
        at += ref.shape[0]

    @pl.loop(0, left.shape[0] // SEG, unroll=4)
    def _(i):
        there = pl.ds(pl.multiple_of(i * wide, wide), wide)
        segments = pl.ds(pl.multiple_of(i * SEG, SEG), SEG)
        for t in range(BINS // LANES):
            re = pl.ds(t * LANES, LANES)
            im = pl.ds(BINS + t * LANES, LANES)
            cross_re = jnp.zeros((wide, LANES), jnp.float32)
            cross_im = jnp.zeros((wide, LANES), jnp.float32)
            rows_re, rows_im = left[segments, re], left[segments, im]
            for s in range(SEG):
                left_re, left_im = rows_re[s : s + 1, :], rows_im[s : s + 1, :]
                right_re = right[t, s * wide : (s + 1) * wide, :]
                right_im = right[t + BINS // LANES, s * wide : (s + 1) * wide, :]
                cross_re = cross_re + (left_re * right_re + left_im * right_im)
                cross_im = cross_im + (left_im * right_re - left_re * right_im)
            cross[there, re] = cross_re
            cross[there, im] = cross_im


def join_kernel(own, other, out):
    out[: own.shape[0], :] = own[...]
    out[own.shape[0] :, :] = other[...]


def join(own, other, cost=10**6):
    return pl.pallas_call(
        join_kernel,
        out_shape=pltpu.VMEM((own.shape[0] + other.shape[0], own.shape[1]), own.dtype),
        in_specs=[VMEM] * 2,
        out_specs=VMEM,
        cost_estimate=pl.CostEstimate(flops=cost, bytes_accessed=cost // 100, transcendentals=0),
        name="join",
    )(in_vmem(own), in_vmem(other))


def correlations(cross, table, out, row_masks):
    count = out.shape[3]
    high, low = split(cross[...])
    both = dot(jnp.concatenate([high, low], axis=0), table[...])
    corr = (both[: high.shape[0]] + both[high.shape[0] :]).astype(jnp.bfloat16)
    row_index = lax.axis_index("row")
    at = 0
    for i in range(out.shape[0]):
        for row_mask in row_masks:
            out[i, 0, row_index ^ row_mask] = corr[at : at + count, :]
            at += count


def prepare_kernel(count, second_parts, first_parts, row_masks, *refs):
    n_second = len(second_parts)
    second_refs = [ref.at[part, :] for ref, part in zip(refs[:n_second], second_parts, strict=True)]
    table, *first_refs, right, ready, left, cross = refs[n_second:]
    first_refs = [ref.at[part, :] for ref, part in zip(first_refs, first_parts, strict=True)]
    wide = count * len(row_masks)
    n = 0
    for ref in second_refs:
        for at in range(0, ref.shape[0], SEG):
            rows = ref[at : at + SEG, :].astype(jnp.float32)
            for t in range(2 * BINS // LANES):
                right[t, pl.ds(n, SEG, stride=wide), :] = rows[:, t * LANES : (t + 1) * LANES]
            n += 1
    cross_spectra(first_refs, left, right, cross, wide)
    correlations(cross, table, ready, row_masks)


def prepare(count, row_masks, second, lags, first):
    n_row = len(row_masks)
    parts = [tuple(part for _, part in blocks) for blocks in (second, first)]
    rows = sum(part.size for part in parts[1])
    return pl.pallas_call(
        functools.partial(prepare_kernel, count, *parts, row_masks),
        out_shape=(
            pltpu.VMEM((2 * BINS // LANES, count * n_row * SEG, LANES), jnp.float32),
            pltpu.VMEM((rows // SEG, 1, n_row, count, LAGS), jnp.bfloat16),
        ),
        in_specs=[VMEM] * (len(second) + 1 + len(first)),
        out_specs=(VMEM, VMEM),
        scratch_shapes=[
            pltpu.VMEM((rows, 2 * BINS), jnp.float32),
            pltpu.VMEM((rows // SEG * count * n_row, 2 * BINS), jnp.float32),
        ],
        name="prepare",
    )(*(in_vmem(block) for block, _ in second), in_vmem(lags), *(in_vmem(block) for block, _ in first))


def stage_kernel(row_masks, right, table, after, *refs):
    *first_refs, ready, left, cross = refs
    cross_spectra(first_refs, left, right, cross, right.shape[1] // SEG)
    correlations(cross, table, ready, row_masks)


def stage(count, row_masks, right, lags, after, first):
    n_row = len(row_masks)
    rows = sum(block.shape[0] for block in first)
    return pl.pallas_call(
        functools.partial(stage_kernel, row_masks),
        out_shape=pltpu.VMEM((rows // SEG, 1, n_row, count, LAGS), jnp.bfloat16),
        in_specs=[VMEM] * (3 + len(first)),
        out_specs=VMEM,
        scratch_shapes=[
            pltpu.VMEM((rows, 2 * BINS), jnp.float32),
            pltpu.VMEM((rows // SEG * count * n_row, 2 * BINS), jnp.float32),
        ],
        name="stage",
    )(*(in_vmem(block) for block in (right, lags, after, *first)))


def correlate_kernel(count, n_ready, masks, bits, row_masks, *refs):
    ready = refs[:n_ready]
    right, table, *first_refs, out, left, cross, last, sent = refs[n_ready:]
    col_index = lax.axis_index("col")
    cols = [at for mask in masks for at in spread(col_index ^ mask, bits)]
    blocks = [
        ref.at[pl.ds(at, count)] for ref in (*ready, last) for at in range(0, ref.shape[0], count)
    ]
    copies = [
        pltpu.make_async_copy(block, out.at[pl.ds(col * count, count)], sent.at[n])
        for n, (block, col) in enumerate(zip(blocks, cols, strict=True))
    ]
    early = len(blocks) - last.shape[0] // count
    for copy in copies[:early]:
        copy.start()
    cross_spectra(first_refs, left, right, cross, count * len(row_masks))
    correlations(cross, table, last, row_masks)
    for copy in copies[early:]:
        copy.start()
    for copy in copies:
        copy.wait()


def correlate(count, n_row, n_col, masks, bits, row_masks, ready, right, lags, first):
    channels, wide = count * n_col, count * n_row
    rows = sum(block.shape[0] for block in first)
    return pl.pallas_call(
        functools.partial(correlate_kernel, count, len(ready), masks, bits, row_masks),
        out_shape=jax.ShapeDtypeStruct((channels, 1, n_row, count, LAGS), jnp.bfloat16),
        in_specs=[VMEM] * (len(ready) + 2 + len(first)),
        out_specs=pl.BlockSpec(memory_space=pl.ANY),
        scratch_shapes=[
            pltpu.VMEM((rows, 2 * BINS), jnp.float32),
            pltpu.VMEM((rows // SEG * wide, 2 * BINS), jnp.float32),
            pltpu.VMEM((rows // SEG, 1, n_row, count, LAGS), jnp.bfloat16),
            pltpu.SemaphoreType.DMA((n_col,)),
        ],
        name="correlate",
    )(*(in_vmem(block) for block in (*ready, right, lags, *first)))


def swap(block, row_mask, col_mask):
    n_row, n_col = lax.axis_size("row"), lax.axis_size("col")
    pairs = [
        (row * n_col + col, (row ^ row_mask) * n_col + (col ^ col_mask))
        for row in range(n_row)
        for col in range(n_col)
    ]
    return lax.ppermute(block, ("row", "col"), pairs)


def spread(col, bits):
    cols = [col]
    for bit in bits:
        cols += [at ^ bit for at in cols]
    return cols


def body(traces, offsets, band_lo, band_hi, live):
    count = traces.shape[0]
    n_row, n_col = lax.axis_size("row"), lax.axis_size("col")
    white = whiten(traces, offsets, band_lo, band_hi, live)
    own, bits = white, []
    bit = n_col // 2
    while bit >= GROUP:
        own = join(own, swap(own, 0, bit))
        bits.append(bit)
        bit //= 2
    far = swap(own, 1, FAR)
    sibling = swap(own, 1, 0)
    across = swap(white, 3, 0)
    pair = join(far, sibling, 10**9)
    near = [swap(pair, 1, step) for step in STEPS]
    other, diagonal = swap(far, 1, 0), swap(across, 1, 0)
    rows, held = white.shape[0], own.shape[0]
    second = [(block, pl.ds(0, rows)) for block in (white, sibling, across, diagonal)]
    row_masks = [0, 1, 3, 2]
    if n_row > len(row_masks):
        stacked = jnp.concatenate([block[part.start : part.start + rows] for block, part in second])
        second = [(stacked, pl.ds(0, stacked.shape[0]))]
        bit = len(row_masks)
        while bit < n_row:
            second += [
                (swap(block, bit, 0), pl.ds(0, block.shape[0])) for block, _ in second
            ]
            row_masks += [mask ^ bit for mask in row_masks]
            bit *= 2
    lags = jnp.asarray(lag_table())
    right, *ready = prepare(count, row_masks, second, lags, [(own, pl.ds(0, held))])
    for blocks in ([other, near[0]], [near[1]]):
        ready += [stage(count, row_masks, right, lags, ready[-1], blocks)]
    masks = [0, FAR] + [mask for step in STEPS for mask in (step ^ FAR, step)]
    return correlate(count, n_row, n_col, masks, bits, row_masks, ready, right, lags, near[2:])


def solution(mesh):
    in_specs = (
        P(("row", "col"), None),
        P(("row", "col"), None),
        P(("row", "col")),
        P(("row", "col")),
        P(("row", "col")),
    )
    out_specs = P("row", "col", None, None, None)
    return jax.shard_map(body, mesh=mesh, in_specs=in_specs, out_specs=out_specs, check_vma=False)
```

```python
import functools
import math

import jax
import jax.numpy as jnp
import numpy as np
from jax import lax
from jax.experimental import pallas as pl
from jax.experimental.pallas import tpu as pltpu
from jax.sharding import PartitionSpec as P

SEG = 8
SAMPLES = 1024
BINS = 256
LAGS = 512
QUARTER = SAMPLES // 4
EIGHTH = SAMPLES // 8
LANES = 128
GROUP = 8
FAR = 4
STEPS = (3, 2, 1)
VMEM = pl.BlockSpec(memory_space=pltpu.VMEM)
SMEM = pl.BlockSpec(memory_space=pltpu.SMEM)


def split(values):
    high = values.astype(jnp.bfloat16)
    return high, (values - high.astype(jnp.float32)).astype(jnp.bfloat16)


def split_table(table):
    high = table.astype(jnp.bfloat16)
    return np.stack([high, (table - high.astype(np.float64)).astype(jnp.bfloat16)])


def eighth_table():
    times = np.arange(EIGHTH)
    freqs = np.arange(BINS) + 1
    phase = (times[:, None] * freqs[None, :] % SAMPLES) * (2.0 * math.pi / SAMPLES)
    return split_table(np.concatenate([np.cos(phase), -np.sin(phase)], axis=1))


def wave_rows():
    times = np.arange(SAMPLES) * (2.0 * math.pi / SAMPLES)
    freqs = np.arange(BINS) + 1
    eighth = (freqs % 8) * (math.pi / 4.0)
    cos_turn = np.array([1.0, 0.0, -1.0, 0.0])[freqs % 4]
    sin_turn = np.array([0.0, 1.0, 0.0, -1.0])[freqs % 4]
    taper = (0.5 - 0.5 * np.cos(times)).reshape(4, QUARTER)
    return np.stack([*taper, cos_turn, sin_turn, np.cos(eighth), np.sin(eighth)]).astype(np.float32)


def lag_table():
    freqs = np.arange(BINS) + 1
    shifts = np.arange(LAGS) - LAGS // 2
    phase = (freqs[:, None] * shifts[None, :] % SAMPLES) * (2.0 * math.pi / SAMPLES)
    table = np.concatenate([np.cos(phase), -np.sin(phase)], axis=0)
    return (table / math.sqrt(SEG * BINS)).astype(jnp.bfloat16)


def in_vmem(array):
    return pltpu.with_memory_space_constraint(array, pltpu.VMEM)


def dot(left, right):
    return jnp.dot(left, right, preferred_element_type=jnp.float32)


def whiten_kernel(offsets, band_lo, band_hi, live, traces, waves, table, out, quarters):
    count = traces.shape[0]
    rows = count * SEG
    for k in range(count):
        for s in range(SEG):
            start = pl.multiple_of(offsets[k, s], QUARTER)
            segment = traces[pl.ds(k, 1), pl.ds(start, SAMPLES)]
            for q in range(4):
                quarters[pl.ds(q * rows + k * SEG + s, 1), :] = segment[
                    :, q * QUARTER : (q + 1) * QUARTER
                ]
    parts = jnp.concatenate(
        [quarters[q * rows : (q + 1) * rows, :] * waves[q : q + 1, :] for q in range(4)], axis=0
    )
    high, low = split(jnp.concatenate([parts[:, :EIGHTH], parts[:, EIGHTH:]], axis=0))
    spectra = dot(
        jnp.concatenate([high, low, high], axis=1),
        jnp.concatenate([table[0], table[0], table[1]], axis=0),
    )
    cos_turn, sin_turn = waves[4:5, :], waves[5:6, :]
    sign = cos_turn * cos_turn - sin_turn * sin_turn

    def turned(n):
        quarter = [spectra[(n + q) * rows : (n + q + 1) * rows] for q in range(4)]
        re, im = [x[:, :BINS] for x in quarter], [x[:, BINS:] for x in quarter]
        return (
            (re[0] + re[2] * sign) + ((re[1] + re[3]) * cos_turn + (im[1] - im[3]) * sin_turn),
            (im[0] + im[2] * sign) + ((im[1] + im[3]) * cos_turn + (re[3] - re[1]) * sin_turn),
        )

    early_re, early_im = turned(0)
    late_re, late_im = turned(4)
    cos_eighth, sin_eighth = waves[6:7, :], waves[7:8, :]
    re = early_re + (late_re * cos_eighth + late_im * sin_eighth)
    im = early_im + (late_im * cos_eighth - late_re * sin_eighth)
    amp = jnp.sqrt(re * re + im * im)
    bins = lax.broadcasted_iota(jnp.int32, (1, BINS), 1)
    total = amp
    for step in (1, 2):
        total = total + jnp.where(bins >= step, pltpu.roll(amp, step, 1), 0.0)
        total = total + jnp.where(bins < BINS - step, pltpu.roll(amp, BINS - step, 1), 0.0)
    level = jnp.sum(amp, axis=1, keepdims=True) * (1.0 / BINS)
    factor = 1.0 / (total / 5.0 + 0.1 * level + 1e-06)
    keep = jnp.concatenate(
        [
            jnp.broadcast_to(
                jnp.where(
                    (bins >= band_lo[k]) & (bins < jnp.where(live[k] == 1, band_hi[k], 0)), 1.0, 0.0
                ),
                (SEG, BINS),
            )
            for k in range(count)
        ],
        axis=0,
    )
    factor = factor * keep
    out[:, :BINS] = (re * factor).astype(jnp.bfloat16)
    out[:, BINS:] = (im * factor).astype(jnp.bfloat16)


def whiten(traces, offsets, band_lo, band_hi, live):
    count = traces.shape[0]
    tables = (wave_rows(), eighth_table())
    return pl.pallas_call(
        whiten_kernel,
        out_shape=pltpu.VMEM((count * SEG, 2 * BINS), jnp.bfloat16),
        in_specs=[SMEM] * 4 + [VMEM] * 3,
        out_specs=VMEM,
        scratch_shapes=[pltpu.VMEM((4 * count * SEG, QUARTER), jnp.float32)],
        name="whiten",
    )(offsets, band_lo, band_hi, live, traces, *(jnp.asarray(table) for table in tables))


def cross_spectra(first_refs, left, right, cross, wide):
    at = 0
    for ref in first_refs:
        left[at : at + ref.shape[0], :] = ref[...].astype(jnp.float32)
        at += ref.shape[0]

    @pl.loop(0, left.shape[0] // SEG, unroll=4)
    def _(i):
        there = pl.ds(pl.multiple_of(i * wide, wide), wide)
        segments = pl.ds(pl.multiple_of(i * SEG, SEG), SEG)
        for t in range(BINS // LANES):
            re = pl.ds(t * LANES, LANES)
            im = pl.ds(BINS + t * LANES, LANES)
            cross_re = jnp.zeros((wide, LANES), jnp.float32)
            cross_im = jnp.zeros((wide, LANES), jnp.float32)
            rows_re, rows_im = left[segments, re], left[segments, im]
            for s in range(SEG):
                left_re, left_im = rows_re[s : s + 1, :], rows_im[s : s + 1, :]
                right_re = right[t, s * wide : (s + 1) * wide, :]
                right_im = right[t + BINS // LANES, s * wide : (s + 1) * wide, :]
                cross_re = cross_re + (left_re * right_re + left_im * right_im)
                cross_im = cross_im + (left_im * right_re - left_re * right_im)
            cross[there, re] = cross_re
            cross[there, im] = cross_im


def join_kernel(own, other, out):
    out[: own.shape[0], :] = own[...]
    out[own.shape[0] :, :] = other[...]


def join(own, other, cost=10**6):
    return pl.pallas_call(
        join_kernel,
        out_shape=pltpu.VMEM((own.shape[0] + other.shape[0], own.shape[1]), own.dtype),
        in_specs=[VMEM] * 2,
        out_specs=VMEM,
        cost_estimate=pl.CostEstimate(flops=cost, bytes_accessed=cost // 100, transcendentals=0),
        name="join",
    )(in_vmem(own), in_vmem(other))


def correlations(cross, table, out, row_masks):
    count = out.shape[3]
    high, low = split(cross[...])
    both = dot(jnp.concatenate([high, low], axis=0), table[...])
    corr = (both[: high.shape[0]] + both[high.shape[0] :]).astype(jnp.bfloat16)
    row_index = lax.axis_index("row")
    at = 0
    for i in range(out.shape[0]):
        for row_mask in row_masks:
            out[i, 0, row_index ^ row_mask] = corr[at : at + count, :]
            at += count


def prepare_kernel(count, second_parts, first_parts, row_masks, *refs):
    n_second = len(second_parts)
    second_refs = [ref.at[part, :] for ref, part in zip(refs[:n_second], second_parts, strict=True)]
    table, *first_refs, right, ready, left, cross = refs[n_second:]
    first_refs = [ref.at[part, :] for ref, part in zip(first_refs, first_parts, strict=True)]
    wide = count * len(row_masks)
    n = 0
    for ref in second_refs:
        for at in range(0, ref.shape[0], SEG):
            rows = ref[at : at + SEG, :].astype(jnp.float32)
            for t in range(2 * BINS // LANES):
                right[t, pl.ds(n, SEG, stride=wide), :] = rows[:, t * LANES : (t + 1) * LANES]
            n += 1
    cross_spectra(first_refs, left, right, cross, wide)
    correlations(cross, table, ready, row_masks)


def prepare(count, row_masks, second, lags, first):
    n_row = len(row_masks)
    parts = [tuple(part for _, part in blocks) for blocks in (second, first)]
    rows = sum(part.size for part in parts[1])
    return pl.pallas_call(
        functools.partial(prepare_kernel, count, *parts, row_masks),
        out_shape=(
            pltpu.VMEM((2 * BINS // LANES, count * n_row * SEG, LANES), jnp.float32),
            pltpu.VMEM((rows // SEG, 1, n_row, count, LAGS), jnp.bfloat16),
        ),
        in_specs=[VMEM] * (len(second) + 1 + len(first)),
        out_specs=(VMEM, VMEM),
        scratch_shapes=[
            pltpu.VMEM((rows, 2 * BINS), jnp.float32),
            pltpu.VMEM((rows // SEG * count * n_row, 2 * BINS), jnp.float32),
        ],
        name="prepare",
    )(*(in_vmem(block) for block, _ in second), in_vmem(lags), *(in_vmem(block) for block, _ in first))


def stage_kernel(row_masks, right, table, after, *refs):
    *first_refs, ready, left, cross = refs
    cross_spectra(first_refs, left, right, cross, right.shape[1] // SEG)
    correlations(cross, table, ready, row_masks)


def stage(count, row_masks, right, lags, after, first):
    n_row = len(row_masks)
    rows = sum(block.shape[0] for block in first)
    return pl.pallas_call(
        functools.partial(stage_kernel, row_masks),
        out_shape=pltpu.VMEM((rows // SEG, 1, n_row, count, LAGS), jnp.bfloat16),
        in_specs=[VMEM] * (3 + len(first)),
        out_specs=VMEM,
        scratch_shapes=[
            pltpu.VMEM((rows, 2 * BINS), jnp.float32),
            pltpu.VMEM((rows // SEG * count * n_row, 2 * BINS), jnp.float32),
        ],
        name="stage",
    )(*(in_vmem(block) for block in (right, lags, after, *first)))


def correlate_kernel(count, n_ready, masks, bits, row_masks, *refs):
    ready = refs[:n_ready]
    right, table, *first_refs, out, left, cross, last, sent = refs[n_ready:]
    col_index = lax.axis_index("col")
    cols = [at for mask in masks for at in spread(col_index ^ mask, bits)]
    blocks = [
        ref.at[pl.ds(at, count)] for ref in (*ready, last) for at in range(0, ref.shape[0], count)
    ]
    copies = [
        pltpu.make_async_copy(block, out.at[pl.ds(col * count, count)], sent.at[n])
        for n, (block, col) in enumerate(zip(blocks, cols, strict=True))
    ]
    early = len(blocks) - last.shape[0] // count
    cross_spectra(first_refs, left, right, cross, count * len(row_masks))
    for copy in copies[:early]:
        copy.start()
    correlations(cross, table, last, row_masks)
    for copy in copies[early:]:
        copy.start()
    for copy in copies:
        copy.wait()


def correlate(count, n_row, n_col, masks, bits, row_masks, ready, right, lags, first):
    channels, wide = count * n_col, count * n_row
    rows = sum(block.shape[0] for block in first)
    return pl.pallas_call(
        functools.partial(correlate_kernel, count, len(ready), masks, bits, row_masks),
        out_shape=jax.ShapeDtypeStruct((channels, 1, n_row, count, LAGS), jnp.bfloat16),
        in_specs=[VMEM] * (len(ready) + 2 + len(first)),
        out_specs=pl.BlockSpec(memory_space=pl.ANY),
        scratch_shapes=[
            pltpu.VMEM((rows, 2 * BINS), jnp.float32),
            pltpu.VMEM((rows // SEG * wide, 2 * BINS), jnp.float32),
            pltpu.VMEM((rows // SEG, 1, n_row, count, LAGS), jnp.bfloat16),
            pltpu.SemaphoreType.DMA((n_col,)),
        ],
        name="correlate",
    )(*(in_vmem(block) for block in (*ready, right, lags, *first)))


def swap(block, row_mask, col_mask):
    n_row, n_col = lax.axis_size("row"), lax.axis_size("col")
    pairs = [
        (row * n_col + col, (row ^ row_mask) * n_col + (col ^ col_mask))
        for row in range(n_row)
        for col in range(n_col)
    ]
    return lax.ppermute(block, ("row", "col"), pairs)


def spread(col, bits):
    cols = [col]
    for bit in bits:
        cols += [at ^ bit for at in cols]
    return cols


def body(traces, offsets, band_lo, band_hi, live):
    count = traces.shape[0]
    n_row, n_col = lax.axis_size("row"), lax.axis_size("col")
    white = whiten(traces, offsets, band_lo, band_hi, live)
    own, bits = white, []
    bit = n_col // 2
    while bit >= GROUP:
        own = join(own, swap(own, 0, bit))
        bits.append(bit)
        bit //= 2
    far = swap(own, 1, FAR)
    sibling = swap(own, 1, 0)
    across = swap(white, 3, 0)
    pair = join(far, sibling, 10**9)
    near = [swap(pair, 1, step) for step in STEPS]
    other, diagonal = swap(far, 1, 0), swap(across, 1, 0)
    rows, held = white.shape[0], own.shape[0]
    second = [(block, pl.ds(0, rows)) for block in (white, sibling, across, diagonal)]
    row_masks = [0, 1, 3, 2]
    if n_row > len(row_masks):
        stacked = jnp.concatenate([block[part.start : part.start + rows] for block, part in second])
        second = [(stacked, pl.ds(0, stacked.shape[0]))]
        bit = len(row_masks)
        while bit < n_row:
            second += [
                (swap(block, bit, 0), pl.ds(0, block.shape[0])) for block, _ in second
            ]
            row_masks += [mask ^ bit for mask in row_masks]
            bit *= 2
    lags = jnp.asarray(lag_table())
    right, *ready = prepare(count, row_masks, second, lags, [(own, pl.ds(0, held))])
    for blocks in ([other, near[0]], [near[1]]):
        ready += [stage(count, row_masks, right, lags, ready[-1], blocks)]
    masks = [0, FAR] + [mask for step in STEPS for mask in (step ^ FAR, step)]
    return correlate(count, n_row, n_col, masks, bits, row_masks, ready, right, lags, near[2:])


def solution(mesh):
    in_specs = (
        P(("row", "col"), None),
        P(("row", "col"), None),
        P(("row", "col")),
        P(("row", "col")),
        P(("row", "col")),
    )
    out_specs = P("row", "col", None, None, None)
    return jax.shard_map(body, mesh=mesh, in_specs=in_specs, out_specs=out_specs, check_vma=False)
```

```python
import functools
import math

import jax
import jax.numpy as jnp
import numpy as np
from jax import lax
from jax.experimental import pallas as pl
from jax.experimental.pallas import tpu as pltpu
from jax.sharding import PartitionSpec as P

SEG = 8
SAMPLES = 1024
BINS = 256
LAGS = 512
QUARTER = SAMPLES // 4
EIGHTH = SAMPLES // 8
LANES = 128
GROUP = 8
FAR = 4
STEPS = (3, 2, 1)
VMEM = pl.BlockSpec(memory_space=pltpu.VMEM)
SMEM = pl.BlockSpec(memory_space=pltpu.SMEM)


def split(values):
    high = values.astype(jnp.bfloat16)
    return high, (values - high.astype(jnp.float32)).astype(jnp.bfloat16)


def split_table(table):
    high = table.astype(jnp.bfloat16)
    return np.stack([high, (table - high.astype(np.float64)).astype(jnp.bfloat16)])


def eighth_table():
    times = np.arange(EIGHTH)
    freqs = np.arange(BINS) + 1
    phase = (times[:, None] * freqs[None, :] % SAMPLES) * (2.0 * math.pi / SAMPLES)
    return split_table(np.concatenate([np.cos(phase), -np.sin(phase)], axis=1))


def wave_rows():
    times = np.arange(SAMPLES) * (2.0 * math.pi / SAMPLES)
    freqs = np.arange(BINS) + 1
    eighth = (freqs % 8) * (math.pi / 4.0)
    cos_turn = np.array([1.0, 0.0, -1.0, 0.0])[freqs % 4]
    sin_turn = np.array([0.0, 1.0, 0.0, -1.0])[freqs % 4]
    taper = (0.5 - 0.5 * np.cos(times)).reshape(4, QUARTER)
    return np.stack([*taper, cos_turn, sin_turn, np.cos(eighth), np.sin(eighth)]).astype(np.float32)


def lag_table():
    freqs = np.arange(BINS) + 1
    shifts = np.arange(LAGS) - LAGS // 2
    phase = (freqs[:, None] * shifts[None, :] % SAMPLES) * (2.0 * math.pi / SAMPLES)
    table = np.concatenate([np.cos(phase), -np.sin(phase)], axis=0)
    return (table / math.sqrt(SEG * BINS)).astype(jnp.bfloat16)


def in_vmem(array):
    return pltpu.with_memory_space_constraint(array, pltpu.VMEM)


def dot(left, right):
    return jnp.dot(left, right, preferred_element_type=jnp.float32)


def whiten_kernel(offsets, band_lo, band_hi, live, traces, waves, table, out, quarters):
    count = traces.shape[0]
    rows = count * SEG
    for k in range(count):
        for s in range(SEG):
            start = pl.multiple_of(offsets[k, s], QUARTER)
            segment = traces[pl.ds(k, 1), pl.ds(start, SAMPLES)]
            for q in range(4):
                quarters[pl.ds(q * rows + k * SEG + s, 1), :] = segment[
                    :, q * QUARTER : (q + 1) * QUARTER
                ]
    parts = jnp.concatenate(
        [quarters[q * rows : (q + 1) * rows, :] * waves[q : q + 1, :] for q in range(4)], axis=0
    )
    high, low = split(jnp.concatenate([parts[:, :EIGHTH], parts[:, EIGHTH:]], axis=0))
    spectra = dot(
        jnp.concatenate([high, low, high], axis=1),
        jnp.concatenate([table[0], table[0], table[1]], axis=0),
    )
    cos_turn, sin_turn = waves[4:5, :], waves[5:6, :]
    sign = cos_turn * cos_turn - sin_turn * sin_turn

    def turned(n):
        quarter = [spectra[(n + q) * rows : (n + q + 1) * rows] for q in range(4)]
        re, im = [x[:, :BINS] for x in quarter], [x[:, BINS:] for x in quarter]
        return (
            (re[0] + re[2] * sign) + ((re[1] + re[3]) * cos_turn + (im[1] - im[3]) * sin_turn),
            (im[0] + im[2] * sign) + ((im[1] + im[3]) * cos_turn + (re[3] - re[1]) * sin_turn),
        )

    early_re, early_im = turned(0)
    late_re, late_im = turned(4)
    cos_eighth, sin_eighth = waves[6:7, :], waves[7:8, :]
    re = early_re + (late_re * cos_eighth + late_im * sin_eighth)
    im = early_im + (late_im * cos_eighth - late_re * sin_eighth)
    amp = jnp.sqrt(re * re + im * im)
    bins = lax.broadcasted_iota(jnp.int32, (1, BINS), 1)
    total = amp
    for step in (1, 2):
        total = total + jnp.where(bins >= step, pltpu.roll(amp, step, 1), 0.0)
        total = total + jnp.where(bins < BINS - step, pltpu.roll(amp, BINS - step, 1), 0.0)
    level = jnp.sum(amp, axis=1, keepdims=True) * (1.0 / BINS)
    factor = 1.0 / (total / 5.0 + 0.1 * level + 1e-06)
    keep = jnp.concatenate(
        [
            jnp.broadcast_to(
                jnp.where(
                    (bins >= band_lo[k]) & (bins < jnp.where(live[k] == 1, band_hi[k], 0)), 1.0, 0.0
                ),
                (SEG, BINS),
            )
            for k in range(count)
        ],
        axis=0,
    )
    factor = factor * keep
    out[:, :BINS] = (re * factor).astype(jnp.bfloat16)
    out[:, BINS:] = (im * factor).astype(jnp.bfloat16)


def whiten(traces, offsets, band_lo, band_hi, live):
    count = traces.shape[0]
    tables = (wave_rows(), eighth_table())
    return pl.pallas_call(
        whiten_kernel,
        out_shape=pltpu.VMEM((count * SEG, 2 * BINS), jnp.bfloat16),
        in_specs=[SMEM] * 4 + [VMEM] * 3,
        out_specs=VMEM,
        scratch_shapes=[pltpu.VMEM((4 * count * SEG, QUARTER), jnp.float32)],
        name="whiten",
    )(offsets, band_lo, band_hi, live, traces, *(jnp.asarray(table) for table in tables))


def cross_spectra(first_refs, left, right, cross, wide):
    at = 0
    for ref in first_refs:
        left[at : at + ref.shape[0], :] = ref[...].astype(jnp.float32)
        at += ref.shape[0]

    @pl.loop(0, left.shape[0] // SEG, unroll=2)
    def _(i):
        there = pl.ds(pl.multiple_of(i * wide, wide), wide)
        segments = pl.ds(pl.multiple_of(i * SEG, SEG), SEG)
        for t in range(BINS // LANES):
            re = pl.ds(t * LANES, LANES)
            im = pl.ds(BINS + t * LANES, LANES)
            cross_re = jnp.zeros((wide, LANES), jnp.float32)
            cross_im = jnp.zeros((wide, LANES), jnp.float32)
            rows_re, rows_im = left[segments, re], left[segments, im]
            for s in range(SEG):
                left_re, left_im = rows_re[s : s + 1, :], rows_im[s : s + 1, :]
                right_re = right[t, s * wide : (s + 1) * wide, :]
                right_im = right[t + BINS // LANES, s * wide : (s + 1) * wide, :]
                cross_re = cross_re + (left_re * right_re + left_im * right_im)
                cross_im = cross_im + (left_im * right_re - left_re * right_im)
            cross[there, re] = cross_re
            cross[there, im] = cross_im


def join_kernel(own, other, out):
    out[: own.shape[0], :] = own[...]
    out[own.shape[0] :, :] = other[...]


def join(own, other, cost=10**6):
    return pl.pallas_call(
        join_kernel,
        out_shape=pltpu.VMEM((own.shape[0] + other.shape[0], own.shape[1]), own.dtype),
        in_specs=[VMEM] * 2,
        out_specs=VMEM,
        cost_estimate=pl.CostEstimate(flops=cost, bytes_accessed=cost // 100, transcendentals=0),
        name="join",
    )(in_vmem(own), in_vmem(other))


def correlations(cross, table, out, row_masks):
    count = out.shape[3]
    high, low = split(cross[...])
    both = dot(jnp.concatenate([high, low], axis=0), table[...])
    corr = (both[: high.shape[0]] + both[high.shape[0] :]).astype(jnp.bfloat16)
    row_index = lax.axis_index("row")
    at = 0
    for i in range(out.shape[0]):
        for row_mask in row_masks:
            out[i, 0, row_index ^ row_mask] = corr[at : at + count, :]
            at += count


def prepare_kernel(count, second_parts, first_parts, row_masks, *refs):
    n_second = len(second_parts)
    second_refs = [ref.at[part, :] for ref, part in zip(refs[:n_second], second_parts, strict=True)]
    table, *first_refs, right, ready, left, cross = refs[n_second:]
    first_refs = [ref.at[part, :] for ref, part in zip(first_refs, first_parts, strict=True)]
    wide = count * len(row_masks)
    n = 0
    for ref in second_refs:
        for at in range(0, ref.shape[0], SEG):
            rows = ref[at : at + SEG, :].astype(jnp.float32)
            for t in range(2 * BINS // LANES):
                right[t, pl.ds(n, SEG, stride=wide), :] = rows[:, t * LANES : (t + 1) * LANES]
            n += 1
    cross_spectra(first_refs, left, right, cross, wide)
    correlations(cross, table, ready, row_masks)


def prepare(count, row_masks, second, lags, first):
    n_row = len(row_masks)
    parts = [tuple(part for _, part in blocks) for blocks in (second, first)]
    rows = sum(part.size for part in parts[1])
    return pl.pallas_call(
        functools.partial(prepare_kernel, count, *parts, row_masks),
        out_shape=(
            pltpu.VMEM((2 * BINS // LANES, count * n_row * SEG, LANES), jnp.float32),
            pltpu.VMEM((rows // SEG, 1, n_row, count, LAGS), jnp.bfloat16),
        ),
        in_specs=[VMEM] * (len(second) + 1 + len(first)),
        out_specs=(VMEM, VMEM),
        scratch_shapes=[
            pltpu.VMEM((rows, 2 * BINS), jnp.float32),
            pltpu.VMEM((rows // SEG * count * n_row, 2 * BINS), jnp.float32),
        ],
        name="prepare",
    )(*(in_vmem(block) for block, _ in second), in_vmem(lags), *(in_vmem(block) for block, _ in first))


def stage_kernel(row_masks, right, table, after, *refs):
    *first_refs, ready, left, cross = refs
    cross_spectra(first_refs, left, right, cross, right.shape[1] // SEG)
    correlations(cross, table, ready, row_masks)


def stage(count, row_masks, right, lags, after, first):
    n_row = len(row_masks)
    rows = sum(block.shape[0] for block in first)
    return pl.pallas_call(
        functools.partial(stage_kernel, row_masks),
        out_shape=pltpu.VMEM((rows // SEG, 1, n_row, count, LAGS), jnp.bfloat16),
        in_specs=[VMEM] * (3 + len(first)),
        out_specs=VMEM,
        scratch_shapes=[
            pltpu.VMEM((rows, 2 * BINS), jnp.float32),
            pltpu.VMEM((rows // SEG * count * n_row, 2 * BINS), jnp.float32),
        ],
        name="stage",
    )(*(in_vmem(block) for block in (right, lags, after, *first)))


def correlate_kernel(count, n_ready, masks, bits, row_masks, *refs):
    ready = refs[:n_ready]
    right, table, *first_refs, out, left, cross, last, sent = refs[n_ready:]
    col_index = lax.axis_index("col")
    cols = [at for mask in masks for at in spread(col_index ^ mask, bits)]
    blocks = [
        ref.at[pl.ds(at, count)] for ref in (*ready, last) for at in range(0, ref.shape[0], count)
    ]
    copies = [
        pltpu.make_async_copy(block, out.at[pl.ds(col * count, count)], sent.at[n])
        for n, (block, col) in enumerate(zip(blocks, cols, strict=True))
    ]
    early = len(blocks) - last.shape[0] // count
    for copy in copies[:early]:
        copy.start()
    cross_spectra(first_refs, left, right, cross, count * len(row_masks))
    correlations(cross, table, last, row_masks)
    for copy in copies[early:]:
        copy.start()
    for copy in copies:
        copy.wait()


def correlate(count, n_row, n_col, masks, bits, row_masks, ready, right, lags, first):
    channels, wide = count * n_col, count * n_row
    rows = sum(block.shape[0] for block in first)
    return pl.pallas_call(
        functools.partial(correlate_kernel, count, len(ready), masks, bits, row_masks),
        out_shape=jax.ShapeDtypeStruct((channels, 1, n_row, count, LAGS), jnp.bfloat16),
        in_specs=[VMEM] * (len(ready) + 2 + len(first)),
        out_specs=pl.BlockSpec(memory_space=pl.ANY),
        scratch_shapes=[
            pltpu.VMEM((rows, 2 * BINS), jnp.float32),
            pltpu.VMEM((rows // SEG * wide, 2 * BINS), jnp.float32),
            pltpu.VMEM((rows // SEG, 1, n_row, count, LAGS), jnp.bfloat16),
            pltpu.SemaphoreType.DMA((n_col,)),
        ],
        name="correlate",
    )(*(in_vmem(block) for block in (*ready, right, lags, *first)))


def swap(block, row_mask, col_mask):
    n_row, n_col = lax.axis_size("row"), lax.axis_size("col")
    pairs = [
        (row * n_col + col, (row ^ row_mask) * n_col + (col ^ col_mask))
        for row in range(n_row)
        for col in range(n_col)
    ]
    return lax.ppermute(block, ("row", "col"), pairs)


def spread(col, bits):
    cols = [col]
    for bit in bits:
        cols += [at ^ bit for at in cols]
    return cols


def body(traces, offsets, band_lo, band_hi, live):
    count = traces.shape[0]
    n_row, n_col = lax.axis_size("row"), lax.axis_size("col")
    white = whiten(traces, offsets, band_lo, band_hi, live)
    own, bits = white, []
    bit = n_col // 2
    while bit >= GROUP:
        own = join(own, swap(own, 0, bit))
        bits.append(bit)
        bit //= 2
    far = swap(own, 1, FAR)
    sibling = swap(own, 1, 0)
    across = swap(white, 3, 0)
    pair = join(far, sibling, 10**9)
    near = [swap(pair, 1, step) for step in STEPS]
    other, diagonal = swap(far, 1, 0), swap(across, 1, 0)
    rows, held = white.shape[0], own.shape[0]
    second = [(block, pl.ds(0, rows)) for block in (white, sibling, across, diagonal)]
    row_masks = [0, 1, 3, 2]
    if n_row > len(row_masks):
        stacked = jnp.concatenate([block[part.start : part.start + rows] for block, part in second])
        second = [(stacked, pl.ds(0, stacked.shape[0]))]
        bit = len(row_masks)
        while bit < n_row:
            second += [
                (swap(block, bit, 0), pl.ds(0, block.shape[0])) for block, _ in second
            ]
            row_masks += [mask ^ bit for mask in row_masks]
            bit *= 2
    lags = jnp.asarray(lag_table())
    right, *ready = prepare(count, row_masks, second, lags, [(own, pl.ds(0, held))])
    for blocks in ([other, near[0]], [near[1]]):
        ready += [stage(count, row_masks, right, lags, ready[-1], blocks)]
    masks = [0, FAR] + [mask for step in STEPS for mask in (step ^ FAR, step)]
    return correlate(count, n_row, n_col, masks, bits, row_masks, ready, right, lags, near[2:])


def solution(mesh):
    in_specs = (
        P(("row", "col"), None),
        P(("row", "col"), None),
        P(("row", "col")),
        P(("row", "col")),
        P(("row", "col")),
    )
    out_specs = P("row", "col", None, None, None)
    return jax.shard_map(body, mesh=mesh, in_specs=in_specs, out_specs=out_specs, check_vma=False)
```
